512 devices in a mesh: dp: 4 (over y), sp: 16 (over z_lo, core), tp: 8 (over z_hi, x).
Axes of the slice: x: 4, y: 4, z: 16 (z_hi: 2, z_lo: 8; z = z_hi * 8 + z_lo), core: 2. Of those that a mesh axis runs over, the one named last changes fastest.
Arguments:
- spatial_input: bfloat16 [4, 16, 256, 1152], P('dp', 'sp'), may hold values from -7 to 7
- out_grad: bfloat16 [4, 16, 256, 1152], P('dp', 'sp'), may hold values from -0.75 to 0.75
- qkv_spatial: bfloat16 [1152, 3, 1152], P(None, None, 'tp'), may hold values from -0.1875 to 0.1875
- out_spatial: bfloat16 [1152, 1152], P('tp'), may hold values from -0.1875 to 0.1875
- qkv_temporal: bfloat16 [1152, 3, 1152], P(None, None, 'tp'), may hold values from -0.1875 to 0.1875
- out_temporal: bfloat16 [1152, 1152], P('tp'), may hold values from -0.1875 to 0.1875
Outputs:
- input_grad: bfloat16 [4, 16, 256, 1152], P('dp', 'sp')
- qkv_spatial_grad: float32 [1152, 3, 1152], P(('sp', 'dp'), None, 'tp')
- out_spatial_grad: float32 [1152, 1152], P('tp', ('sp', 'dp'))
- qkv_temporal_grad: float32 [1152, 3, 1152], P(('sp', 'dp'), None, 'tp')
- out_temporal_grad: float32 [1152, 1152], P('tp', ('sp', 'dp'))
The draws below stay inside these ranges and needn't reach their ends.
All inputs are finite; a program needn't handle non-finite values.
Results may differ from the reference program's by a relative error of at most 0.035.
Values may be sent and summed in bfloat16 or wider, within the bound.
A program may use at most 64 MiB of HBM per device.

```python
import jax
import jax.numpy as jnp
from jax import lax

D = 1152
HEADS = 16
HEAD_DIM = 72
FRAMES = 16
PATCHES = 256
VIDEOS = 4
N_SP = 16
N_TP = 8


def draw_spatial_input(key, part):
    key = jax.random.fold_in(key, 11)
    full_shape = (VIDEOS, FRAMES, PATCHES, D)
    values = jax.random.truncated_normal(key, -6.0, 6.0, full_shape, jnp.float32)
    return values.astype(jnp.bfloat16)


def block_levels(rng, shape, cuts, smallest, largest):
    factor_of = 1.0
    for dim, blocks in cuts:
        draws = jax.random.uniform(jax.random.fold_in(jax.random.fold_in(rng, 6), dim), (blocks,), jnp.float32, smallest / len(cuts), largest / len(cuts))
        factor_of = factor_of * jnp.repeat(jnp.exp(draws), shape[dim] // blocks).reshape((-1,) + (1,) * (len(shape) - 1 - dim))
    return factor_of


def normal_values(key, dims, scale, reach, shards=(), kind=jnp.bfloat16):
    gain = block_levels(key, dims, shards, -0.22, 0.18) if shards else 1.0
    array = jax.random.normal(key, dims, jnp.float32) * scale * gain
    return jnp.minimum(jnp.maximum(array, -reach), reach).astype(kind)


def setup_inputs(seed: int = 0) -> dict:
    arg_keys = jax.random.split(jax.random.key(seed), 7)
    spatial_input = draw_spatial_input(jax.random.fold_in(arg_keys[6], 71), 0)
    out_grad = normal_values(arg_keys[1], (VIDEOS, FRAMES, PATCHES, D), 0.125, 0.75, ((0, 4), (1, 16)))
    qkv_spatial = normal_values(arg_keys[2], (D, 3, HEADS * HEAD_DIM), D ** -0.5, 0.1875, ((2, 8),))
    out_spatial = normal_values(arg_keys[3], (HEADS * HEAD_DIM, D), (HEADS * HEAD_DIM) ** -0.5, 0.1875, ((0, 8),))
    qkv_temporal = normal_values(arg_keys[4], (D, 3, HEADS * HEAD_DIM), D ** -0.5, 0.1875, ((2, 8),))
    out_temporal = normal_values(arg_keys[5], (HEADS * HEAD_DIM, D), (HEADS * HEAD_DIM) ** -0.5, 0.1875, ((0, 8),))
    return {"spatial_input": spatial_input, "out_grad": out_grad, "qkv_spatial": qkv_spatial, "out_spatial": out_spatial, "qkv_temporal": qkv_temporal, "out_temporal": out_temporal}


def project(tokens, weight):
    token_rows = tokens.reshape(-1, tokens.shape[-1])
    flat_rows = jnp.dot(token_rows, weight.reshape(weight.shape[0], -1), preferred_element_type=jnp.float32)
    packed = flat_rows.astype(jnp.bfloat16).reshape(tokens.shape[0], tokens.shape[1], 3, -1, HEAD_DIM)
    return packed[:, :, 0], packed[:, :, 1], packed[:, :, 2]


def attend(queries, key_rows, value_rows):
    factor = HEAD_DIM ** -0.5
    scores = jnp.einsum("blhe,bmhe->bhlm", queries.astype(jnp.float32), key_rows.astype(jnp.float32)) * factor
    softmax_rows = jax.nn.softmax(scores, axis=-1)
    weights = softmax_rows.astype(jnp.bfloat16)
    mixed_rows = jnp.einsum("bhlm,bmhe->blhe", weights.astype(jnp.float32), value_rows.astype(jnp.float32))
    return softmax_rows, weights, mixed_rows.astype(jnp.bfloat16)


def attend_back(queries, key_rows, value_rows, softmax_rows, weights, grad_mixed):
    factor = HEAD_DIM ** -0.5
    grad_wide = grad_mixed.astype(jnp.float32)
    grad_values = jnp.einsum("bhlm,blhe->bmhe", weights.astype(jnp.float32), grad_wide)
    grad_probs = jnp.einsum("blhe,bmhe->bhlm", grad_wide, value_rows.astype(jnp.float32))
    centre = jnp.sum(grad_probs * softmax_rows, axis=-1, keepdims=True)
    grad_scores = (softmax_rows * (grad_probs - centre) * factor).astype(jnp.bfloat16)
    grad_queries = jnp.einsum("bhlm,bmhe->blhe", grad_scores.astype(jnp.float32), key_rows.astype(jnp.float32))
    grad_keys = jnp.einsum("bhlm,blhe->bmhe", grad_scores.astype(jnp.float32), queries.astype(jnp.float32))
    return jnp.stack([grad_queries, grad_keys, grad_values], axis=2).astype(jnp.bfloat16)


def rounded_sum(pieces):
    rounded = lax.optimization_barrier(pieces.astype(jnp.bfloat16))
    return jnp.sum(rounded.astype(jnp.float32), axis=1)


def group_out(mixed_rows, weight):
    group_width = weight.shape[0] // N_TP
    left_rows = mixed_rows.reshape(mixed_rows.shape[0], N_TP, group_width).astype(jnp.float32)
    right_rows = weight.reshape(N_TP, group_width, -1).astype(jnp.float32)
    return rounded_sum(jnp.einsum("ngc,gcd->ngd", left_rows, right_rows))


def group_back(grad_rows, weight):
    group_width = weight.shape[2] // N_TP
    left_rows = grad_rows.reshape(grad_rows.shape[0], 3, N_TP, group_width).astype(jnp.float32)
    right_rows = weight.reshape(weight.shape[0], 3, N_TP, group_width).astype(jnp.float32)
    return rounded_sum(jnp.einsum("ncgk,dcgk->ngd", left_rows, right_rows))


def block_terms(left_rows, right_rows):
    def accumulate(running, operands):
        block_term = jnp.dot(operands[0].T, operands[1], preferred_element_type=jnp.float32)
        rounded = lax.optimization_barrier(block_term.astype(jnp.bfloat16))
        return running + rounded.astype(jnp.float32), None

    start_sum = jnp.zeros((left_rows.shape[2], right_rows.shape[2]), jnp.float32)
    running, _ = lax.scan(accumulate, start_sum, (left_rows, right_rows))
    return running


def per_video(spatial_in, grad_out, qkv_spatial, out_spatial, qkv_temporal, out_temporal):
    frames, patches, model_width = spatial_in.shape
    queries, key_rows, value_rows = project(spatial_in, qkv_spatial)
    softmax_s, weights_s, mixed_s = attend(queries, key_rows, value_rows)
    flat_s = mixed_s.reshape(frames * patches, -1)
    spatial_rows = spatial_in.reshape(-1, model_width)
    temporal_in = (spatial_rows.astype(jnp.float32) + group_out(flat_s, out_spatial)).astype(jnp.bfloat16)
    temporal_seq = temporal_in.reshape(frames, patches, model_width).transpose(1, 0, 2)
    grad_rows = grad_out.transpose(1, 0, 2).reshape(-1, model_width)
    queries_t, key_rows_t, value_rows_t = project(temporal_seq, qkv_temporal)
    softmax_t, weights_t, mixed_t = attend(queries_t, key_rows_t, value_rows_t)
    columns = flat_s.shape[1]
    frame_mixed_t = mixed_t.reshape(patches, frames, columns).transpose(1, 0, 2)
    grad_mixed_t = jnp.dot(grad_rows, out_temporal.T, preferred_element_type=jnp.float32).astype(jnp.bfloat16)
    grads_t = attend_back(queries_t, key_rows_t, value_rows_t, softmax_t, weights_t, grad_mixed_t.reshape(mixed_t.shape))
    flat_grads_t = grads_t.reshape(patches * frames, 3, -1)
    temporal_grad = (grad_rows.astype(jnp.float32) + group_back(flat_grads_t, qkv_temporal)).astype(jnp.bfloat16)
    temporal_grad_s = temporal_grad.reshape(patches, frames, model_width).transpose(1, 0, 2).reshape(-1, model_width)
    grad_mixed_s = jnp.dot(temporal_grad_s, out_spatial.T, preferred_element_type=jnp.float32).astype(jnp.bfloat16)
    grads_s = attend_back(queries, key_rows, value_rows, softmax_s, weights_s, grad_mixed_s.reshape(mixed_s.shape))
    flat_grads_s = grads_s.reshape(frames * patches, 3, -1)
    input_grad = (temporal_grad_s.astype(jnp.float32) + group_back(flat_grads_s, qkv_spatial)).astype(jnp.bfloat16)
    qkv_s_sum = block_terms(spatial_rows.reshape(N_SP, -1, model_width), flat_grads_s.reshape(N_SP, -1, 3 * columns))
    out_s_sum = block_terms(flat_s.reshape(N_SP, -1, columns), temporal_grad_s.reshape(N_SP, -1, model_width))
    qkv_t_sum = block_terms(temporal_seq.reshape(N_SP, -1, model_width), flat_grads_t.reshape(N_SP, -1, 3 * columns))
    out_t_sum = block_terms(frame_mixed_t.reshape(N_SP, -1, columns), grad_out.reshape(N_SP, -1, model_width))
    return (input_grad.reshape(frames, patches, model_width), qkv_s_sum.reshape(model_width, 3, columns), out_s_sum,
            qkv_t_sum.reshape(model_width, 3, columns), out_t_sum)


def reference(spatial_input, out_grad, qkv_spatial, out_spatial, qkv_temporal, out_temporal):
    def one_video(operands):
        return per_video(operands[0], operands[1], qkv_spatial, out_spatial, qkv_temporal, out_temporal)

    input_grad, qkv_s_all, out_s_all, qkv_t_all, out_t_all = lax.map(one_video, (spatial_input, out_grad))
    return (input_grad, jnp.sum(qkv_s_all, axis=0), jnp.sum(out_s_all, axis=0),
            jnp.sum(qkv_t_all, axis=0), jnp.sum(out_t_all, axis=0))
```

```python
import functools

import jax
import jax.numpy as jnp
import numpy as np
from jax import lax
from jax.experimental import pallas as pl
from jax.experimental.pallas import tpu as pltpu
from jax.sharding import PartitionSpec as P

HEAD_DIM = 72
LANES = 128
ROWS = 16
MESH = pl.DeviceIdType.MESH
F32, BF16 = jnp.float32, jnp.bfloat16


def dot_nn(left, right):
    return lax.dot_general(left, right, (((1,), (0,)), ((), ())), preferred_element_type=F32)


def dot_nt(left, right):
    return lax.dot_general(left, right, (((1,), (1,)), ((), ())), preferred_element_type=F32)


def dot_tn(left, right):
    return lax.dot_general(left, right, (((0,), (0,)), ((), ())), preferred_element_type=F32)


class Sizes:
    def __init__(self, mesh_shape, tokens, width):
        self.ny, self.ns = mesh_shape["dp"], mesh_shape["sp"]
        self.nx = mesh_shape["tp"] // 2
        self.nzl = self.ns // 2
        self.tokens, self.width = tokens, width
        self.tiles = width // LANES
        self.reg = self.tiles // self.nx
        assert self.tiles == self.reg * self.nx + 1
        self.per = self.ns // self.nx
        self.cols = 2 * HEAD_DIM
        self.wide = -(-(4 * self.cols) // LANES) * LANES
        self.core_rows = width // 2
        self.y_rows = self.core_rows // self.ny
        self.rr = width // (self.ns * self.ny)
        self.rp = -(-self.rr // 16) * 16


def row_order(z):
    order = np.arange(z.width).reshape(z.nzl, 2, z.ny, z.rr).transpose(1, 2, 0, 3).reshape(-1)
    onehot = np.zeros((z.width, z.width), np.float32)
    onehot[np.arange(z.width), order] = 1.0
    return onehot.astype(jnp.bfloat16)


def row_pad(z):
    onehot = np.zeros((z.nzl * z.rp, z.y_rows), np.float32)
    for chip in range(z.nzl):
        for row in range(z.rr):
            onehot[chip * z.rp + row, chip * z.rr + row] = 1.0
    return onehot.astype(jnp.bfloat16)


def kernel(
    z,
    x_ref, go_ref, ws_ref, wos_ref, wt_ref, wot_ref, order_ref, pad_ref,
    out_ref, wt_out, ws_out,
    qkv_s, qkv_t, prob_s, prob_t, mix_s, mix_t, gm_t, grads,
    pb, rx, sb, zb, ze, eb,
    ti, tie, tig, tg, tge, tgg, got, ge, geg,
    lt_x, lt_ti, lt_go, lt_tg,
    term, term_in, yb, yr, zw, zr,
    rx_s, rx_r, zb_s, zb_r, ag_s, ag_r, go_s, go_r, gag_s, gag_r, eb_s, eb_r,
    w_s, w_r,
):
    n = z.tokens
    cols = z.cols
    factor = HEAD_DIM ** (-0.5)
    dp, s, t = lax.axis_index("dp"), lax.axis_index("sp"), lax.axis_index("tp")
    zh, xi = t // z.nx, t % z.nx
    zl, core = s // 2, s % 2
    owner = s % z.nx
    is_owner = xi == owner
    last = pl.ds((z.tiles - 1) * LANES, LANES)

    def at_x(k):
        return (dp, s, zh * z.nx + (xi + k + 1) % z.nx)

    def at_z(i):
        place = (zh * z.ns + s + i) % (2 * z.ns)
        return place % z.ns, (dp, place % z.ns, (place // z.ns) * z.nx + xi)

    def send(src, dst, ssem, rsem, dev):
        pltpu.make_async_remote_copy(
            src_ref=src, dst_ref=dst, send_sem=ssem, recv_sem=rsem, device_id=dev, device_id_type=MESH
        ).start()

    def wait(ref, sem):
        pltpu.make_async_copy(ref, ref, sem).wait()

    def tile_lanes(who, j, count=1):
        return pl.ds(pl.multiple_of((who * z.reg + j) * LANES, LANES), count * LANES)

    def rows_of(i, base=0):
        return pl.ds(pl.multiple_of(base + i * ROWS, ROWS), ROWS)

    barrier = pltpu.get_barrier_semaphore()
    for k in range(z.nx - 1):
        pl.semaphore_signal(barrier, inc=1, device_id=at_x(k), device_id_type=MESH)
    for k in range(z.ny - 1):
        pl.semaphore_signal(barrier, inc=1, device_id=((dp + k + 1) % z.ny, s, t), device_id_type=MESH)

    def greet(i, carry):
        pl.semaphore_signal(barrier, inc=1, device_id=at_z(i)[1], device_id_type=MESH)
        return carry

    lax.fori_loop(1, 2 * z.ns, greet, 0)
    pl.semaphore_wait(barrier, (z.nx - 1) + (z.ny - 1) + (2 * z.ns - 1))

    def send_go(i, carry):
        to = (s + i) % z.ns
        send(
            go_ref.at[rows_of(to), tile_lanes(xi, 0, z.reg)],
            got.at[rows_of(s), tile_lanes(xi, 0, z.reg)],
            go_s.at[0], go_r.at[0], (dp, to, t),
        )
        return carry

    def send_go_last(i, carry):
        to = (s + i) % z.ns
        send(go_ref.at[rows_of(to), last], ge.at[rows_of(s // z.nx)], go_s.at[1], go_r.at[1], (dp, to, t))
        return carry

    pltpu.make_async_copy(
        go_ref.at[rows_of(s), tile_lanes(xi, 0, z.reg)], got.at[rows_of(s), tile_lanes(xi, 0, z.reg)], go_r.at[0]
    ).start()
    lax.fori_loop(1, z.ns, send_go, 0)

    @pl.when(is_owner)
    def _():
        pltpu.make_async_copy(go_ref.at[rows_of(s), last], ge.at[rows_of(s // z.nx)], go_r.at[1]).start()
        lax.fori_loop(1, z.ns, send_go_last, 0)

    first_head = lax.broadcasted_iota(jnp.int32, (n, cols), 1) < HEAD_DIM

    def one_head(rows, h):
        keep = first_head if h == 0 else jnp.logical_not(first_head)
        return jnp.where(keep, rows.astype(F32), 0.0).astype(BF16)

    def both_heads(pair):
        return jnp.where(first_head, pair[0], pair[1])

    def project(rows, weight_ref, qkv_ref):
        for part in range(3):
            qkv_ref[part] = dot_nt(rows, weight_ref[part * cols : (part + 1) * cols, :]).astype(BF16)

    def attend(qkv_ref, prob_ref, mix_ref, same):
        q, k, v = qkv_ref[0], qkv_ref[1], qkv_ref[2]
        mixed = []
        for h in range(2):
            scores = dot_nt(one_head(q, h), k) * factor
            if same is not None:
                scores = jnp.where(same, scores, -1e30)
            e = jnp.exp(scores - jnp.max(scores, axis=-1, keepdims=True))
            probs = e / jnp.sum(e, axis=-1, keepdims=True)
            prob_ref[h] = probs
            mixed.append(dot_nn(probs.astype(BF16), v))
        mix_ref[...] = both_heads(mixed).astype(BF16)

    def attend_back(qkv_ref, prob_ref, grad_mixed, grads_ref):
        q, k, v = qkv_ref[0], qkv_ref[1], qkv_ref[2]
        dq, dk, dv = [], [], []
        for h in range(2):
            probs = prob_ref[h]
            dp_ = dot_nt(one_head(grad_mixed, h), v)
            centre = jnp.sum(dp_ * probs, axis=-1, keepdims=True)
            ds = (probs * (dp_ - centre) * factor).astype(BF16)
            dq.append(dot_nn(ds, k))
            dk.append(dot_tn(ds, q))
            dv.append(dot_tn(probs.astype(BF16), grad_mixed))
        for part, pair in enumerate((dq, dk, dv)):
            grads_ref[part] = both_heads(pair).astype(BF16)

    def transposed(rows_ref, lt_ref):
        step = 192 if z.width % 192 == 0 else 160

        def one(i, carry):
            at = pl.ds(pl.multiple_of(i * step, 16), step)
            lt_ref[at, :] = dot_nt(order_ref[at, :], rows_ref[...]).astype(BF16)
            return carry

        lax.fori_loop(0, z.width // step, one, 0)

    def send_x(p, j):
        for k in range(z.nx - 1):
            to = (xi + k + 1) % z.nx
            send(pb.at[p, :, tile_lanes(to, j)], rx.at[p, j, k], rx_s.at[p, j], rx_r.at[p, j], at_x(k))

    def send_x_last(p):
        @pl.when(jnp.logical_not(is_owner))
        def _():
            k = (owner - xi - 1 + z.nx) % z.nx
            send(
                pb.at[p, :, last], rx.at[p, z.reg, k], rx_s.at[p, z.reg], rx_r.at[p, z.reg],
                (dp, s, zh * z.nx + owner),
            )

    def partial_and_send(p, product):
        for j in range(z.reg):
            for who in range(z.nx):
                lanes = slice((who * z.reg + j) * LANES, (who * z.reg + j + 1) * LANES)
                pb[p, :, lanes] = product(lanes).astype(BF16)
            send_x(p, j)
        lanes = slice((z.tiles - 1) * LANES, z.tiles * LANES)
        pb[p, :, lanes] = product(lanes).astype(BF16)
        send_x_last(p)

    def sum_x(p, j, extra=None):
        wait(rx.at[p, j], rx_r.at[p, j])
        lanes = tile_lanes(xi, j) if j < z.reg else last
        total = pb[p, :, lanes].astype(F32)
        for k in range(z.nx - 1):
            total += rx[p, j, k].astype(F32)
        if extra is not None:
            total += extra(lanes)
        sb[p, j] = total.astype(BF16)

    def send_z(p, j):
        if j < z.reg:
            pltpu.make_async_copy(sb.at[p, j, rows_of(s)], zb.at[p, j, rows_of(s, zh * n)], zb_r.at[p, j]).start()
        else:
            pltpu.make_async_copy(
                sb.at[p, j, rows_of(s)], ze.at[p, rows_of(s // z.nx, zh * z.per * ROWS)], zb_r.at[p, j]
            ).start()

        def one(i, carry):
            to, dev = at_z(i)
            dst = zb.at[p, j, rows_of(s, zh * n)] if j < z.reg else ze.at[p, rows_of(s // z.nx, zh * z.per * ROWS)]
            send(sb.at[p, j, rows_of(to)], dst, zb_s.at[p, j], zb_r.at[p, j], dev)
            return carry

        lax.fori_loop(1, 2 * z.ns, one, 0)

    def switch(p, extra=None):
        for j in range(z.reg):
            sum_x(p, j, extra)
            send_z(p, j)

        @pl.when(is_owner)
        def _():
            sum_x(p, z.reg, extra)
            send_z(p, z.reg)

    def sum_z(p, full, mine, others, extra=None):
        for j in range(z.reg):
            wait(zb.at[p, j], zb_r.at[p, j])
            lanes = tile_lanes(xi, j)
            total = zb[p, j, 0:n].astype(F32) + zb[p, j, n : 2 * n].astype(F32)
            if extra is not None:
                total += extra[:, lanes].astype(F32)
            full[:, lanes] = total.astype(BF16)
            for k in range(z.nx - 1):
                send(full.at[:, lanes], full.at[:, lanes], ag_s.at[p, j], ag_r.at[p, j, k], at_x(k))
        wait(ze.at[p], zb_r.at[p, z.reg])
        half = z.per * ROWS
        for i in range(z.per):
            total = ze[p, i * ROWS : (i + 1) * ROWS].astype(F32)
            total += ze[p, half + i * ROWS : half + (i + 1) * ROWS].astype(F32)
            if extra is not None:
                total += extra[rows_of(xi + z.nx * i), last].astype(F32)
            mine[i * ROWS : (i + 1) * ROWS, :] = total.astype(BF16)
        for k in range(z.nx - 1):
            send(mine, others.at[k], ag_s.at[p, z.reg], ag_r.at[p, z.reg, k], at_x(k))

    def place_last(full, block, who):
        for i in range(z.per):
            full[rows_of(who + z.nx * i), last] = block[i * ROWS : (i + 1) * ROWS, :]

    def gather_x(p, full, mine, others):
        place_last(full, mine, xi)
        for k in range(z.nx - 1):
            who = (xi - k - 1 + z.nx) % z.nx
            for j in range(z.reg):
                wait(full.at[:, tile_lanes(who, j)], ag_r.at[p, j, k])
            wait(others.at[k], ag_r.at[p, z.reg, k])
            place_last(full, others.at[k], who)

    def weight_terms(b, lt_qkv, lt_out, mix_ref):
        tail = z.wide - LANES * (3 * cols // LANES)
        base = z.wide - tail
        packed = jnp.concatenate(
            [grads[b, 0], grads[b, 1], grads[b, 2], jnp.zeros((n, z.wide - 3 * cols), BF16)], axis=1
        )
        placed = jnp.concatenate(
            [jnp.zeros((n, 3 * cols - base), BF16), mix_ref[...], jnp.zeros((n, z.wide - 4 * cols), BF16)], axis=1
        )
        step = 192 if z.width % 192 == 0 else 160

        def one(i, carry):
            at = pl.ds(pl.multiple_of(i * step, 16), step)
            left, left_out = lt_qkv[at, :], lt_out[at, :]
            term[b, at, 0:base] = dot_nn(left, packed[:, 0:base]).astype(BF16)
            term[b, at, base : z.wide] = (dot_nn(left, packed[:, base:]) + dot_nn(left_out, placed)).astype(BF16)
            return carry

        lax.fori_loop(0, z.width // step, one, 0)
        away = pl.ds(pl.multiple_of((1 - core) * z.core_rows, 16), z.core_rows)
        send(term.at[b, away], term_in.at[b], w_s.at[b, 0], w_r.at[b, 0], (dp, s + 1 - 2 * core, t))

    def weights_y(b):
        wait(term_in.at[b], w_r.at[b, 0])
        here = pl.ds(pl.multiple_of(core * z.core_rows, 16), z.core_rows)
        yb[b] = (term[b, here].astype(F32) + term_in[b].astype(F32)).astype(BF16)
        for k in range(z.ny - 1):
            to = (dp + k + 1) % z.ny
            src = yb.at[b, pl.ds(pl.multiple_of(to * z.y_rows, 16), z.y_rows)]
            send(src, yr.at[b, k], w_s.at[b, 1], w_r.at[b, 1], (to, s, t))

    def weights_z(b):
        wait(yr.at[b], w_r.at[b, 1])
        total = yb[b, pl.ds(pl.multiple_of(dp * z.y_rows, 16), z.y_rows)].astype(F32)
        for k in range(z.ny - 1):
            total += yr[b, k].astype(F32)
        zw[b] = dot_nn(pad_ref[...], total.astype(BF16)).astype(BF16)

        def block(i):
            return pl.ds(pl.multiple_of(i * z.rp, 16), z.rp)

        pltpu.make_async_copy(zw.at[b, block(zl)], zr.at[b, zl], w_r.at[b, 2]).start()
        for k in range(z.nzl - 1):
            to = (zl + k + 1) % z.nzl
            send(zw.at[b, block(to)], zr.at[b, zl], w_s.at[b, 2], w_r.at[b, 2], (dp, 2 * to + core, t))

    def weights_end(b, w_out):
        wait(zr.at[b], w_r.at[b, 2])
        total = zr[b, 0].astype(F32)
        for k in range(1, z.nzl):
            total += zr[b, k].astype(F32)
        w_out[...] = total

    project(x_ref[...], ws_ref, qkv_s)
    attend(qkv_s, prob_s, mix_s, None)
    partial_and_send(0, lambda lanes: dot_nn(mix_s[...], wos_ref[:, lanes]))

    def add_input(lanes):
        return x_ref[:, lanes].astype(F32) * jnp.where(zh == 0, 1.0, 0.0)

    switch(0, add_input)

    wait(got.at[:, tile_lanes(xi, 0, z.reg)], go_r.at[0])
    wait(ge, go_r.at[1])
    for k in range(z.nx - 1):
        lanes = tile_lanes(xi, 0, z.reg)
        send(got.at[:, lanes], got.at[:, lanes], gag_s.at[0], gag_r.at[0, k], at_x(k))
        send(ge, geg.at[k], gag_s.at[1], gag_r.at[1, k], at_x(k))
    transposed(x_ref, lt_x)

    sum_z(0, ti, tie, tig)

    place_last(got, ge, xi)
    for k in range(z.nx - 1):
        who = (xi - k - 1 + z.nx) % z.nx
        wait(got.at[:, tile_lanes(who, 0, z.reg)], gag_r.at[0, k])
        wait(geg.at[k], gag_r.at[1, k])
        place_last(got, geg.at[k], who)
    gm_t[...] = dot_nt(got[...], wot_ref[...]).astype(BF16)
    transposed(got, lt_go)
    gather_x(0, ti, tie, tig)

    rows_i = lax.broadcasted_iota(jnp.int32, (n, n), 0)
    cols_i = lax.broadcasted_iota(jnp.int32, (n, n), 1)
    same = (rows_i & (ROWS - 1)) == (cols_i & (ROWS - 1))
    project(ti[...], wt_ref, qkv_t)
    attend(qkv_t, prob_t, mix_t, same)
    attend_back(qkv_t, prob_t, gm_t[...], grads.at[0])

    def back(b, weight_ref):
        def product(lanes):
            total = dot_nn(grads[b, 0], weight_ref[0:cols, lanes])
            for part in range(1, 3):
                total += dot_nn(grads[b, part], weight_ref[part * cols : (part + 1) * cols, lanes])
            return total

        return product

    partial_and_send(1, back(0, wt_ref))
    transposed(ti, lt_ti)
    weight_terms(0, lt_ti, lt_go, mix_t)
    switch(1)
    weights_y(0)
    sum_z(1, tg, tge, tgg, go_ref)
    weights_z(0)
    gather_x(1, tg, tge, tgg)

    grad_mixed_s = dot_nt(tg[...], wos_ref[...]).astype(BF16)
    attend_back(qkv_s, prob_s, grad_mixed_s, grads.at[1])
    partial_and_send(2, back(1, ws_ref))
    transposed(tg, lt_tg)
    weight_terms(1, lt_x, lt_tg, mix_s)

    def exchange(j):
        sum_x(2, j)
        send(sb.at[2, j], eb.at[j], eb_s.at[j], eb_r.at[j], (dp, s, (1 - zh) * z.nx + xi))

    def finish(j, k_sem):
        wait(eb.at[j], eb_r.at[j])
        lanes = tile_lanes(xi, j) if j < z.reg else last
        total = tg[:, lanes].astype(F32) + (sb[2, j].astype(F32) + eb[j].astype(F32))
        out_ref[:, lanes] = total.astype(BF16)
        for k in range(z.nx - 1):
            send(out_ref.at[:, lanes], out_ref.at[:, lanes], ag_s.at[2, j], ag_r.at[2, j, k_sem(k)], at_x(k))

    for j in range(z.reg):
        exchange(j)

    @pl.when(is_owner)
    def _():
        exchange(z.reg)

    weights_y(1)
    for j in range(z.reg):
        finish(j, lambda k: k)

    @pl.when(is_owner)
    def _():
        finish(z.reg, lambda k: 0)

    weights_z(1)
    weights_end(0, wt_out)
    for k in range(z.nx - 1):
        who = (xi - k - 1 + z.nx) % z.nx
        for j in range(z.reg):
            wait(out_ref.at[:, tile_lanes(who, j)], ag_r.at[2, j, k])

    @pl.when(jnp.logical_not(is_owner))
    def _():
        wait(out_ref.at[:, last], ag_r.at[2, z.reg, 0])

    weights_end(1, ws_out)

    for p in range(3):
        for j in range(z.reg):
            wait(rx.at[p, j], rx_s.at[p, j])
            wait(rx.at[p, j], ag_s.at[p, j])

        @pl.when(jnp.logical_not(is_owner))
        def _():
            wait(rx.at[p, z.reg, 0], rx_s.at[p, z.reg])

    sent = (2 * z.ns - 1) * ROWS
    for p in range(2):
        for j in range(z.reg):
            wait(zb.at[p, j, pl.ds(0, sent)], zb_s.at[p, j])
        wait(tig if p == 0 else tgg, ag_s.at[p, z.reg])

        @pl.when(is_owner)
        def _():
            wait(zb.at[p, 0, pl.ds(0, sent)], zb_s.at[p, z.reg])

    for j in range(z.reg):
        wait(eb.at[j], eb_s.at[j])

    @pl.when(is_owner)
    def _():
        wait(eb.at[z.reg], eb_s.at[z.reg])
        wait(rx.at[2, z.reg], ag_s.at[2, z.reg])
        wait(got.at[pl.ds(0, (z.ns - 1) * ROWS), last], go_s.at[1])

    wait(got.at[pl.ds(0, (z.ns - 1) * ROWS), pl.ds(0, z.reg * LANES)], go_s.at[0])
    wait(got.at[:, pl.ds(0, (z.nx - 1) * z.reg * LANES)], gag_s.at[0])
    wait(geg, gag_s.at[1])
    for b in range(2):
        wait(term_in.at[b], w_s.at[b, 0])
        wait(yr.at[b], w_s.at[b, 1])
        wait(zr.at[b, pl.ds(0, z.nzl - 1)], w_s.at[b, 2])


def run(z, *arrays):
    n, width, cols = z.tokens, z.width, z.cols
    chunks = z.reg + 1
    dma = pltpu.SemaphoreType.DMA
    vmem = pltpu.VMEM
    shared = z.per * ROWS
    return pl.pallas_call(
        functools.partial(kernel, z),
        out_shape=(
            jax.ShapeDtypeStruct((n, width), BF16),
            jax.ShapeDtypeStruct((z.rp, z.wide), F32),
            jax.ShapeDtypeStruct((z.rp, z.wide), F32),
        ),
        in_specs=[pl.BlockSpec(memory_space=pltpu.VMEM)] * len(arrays),
        out_specs=[pl.BlockSpec(memory_space=pltpu.VMEM)] * 3,
        scratch_shapes=[
            vmem((3, n, cols), BF16), vmem((3, n, cols), BF16),
            vmem((2, n, n), F32), vmem((2, n, n), F32),
            vmem((n, cols), BF16), vmem((n, cols), BF16), vmem((n, cols), BF16),
            vmem((2, 3, n, cols), BF16),
            vmem((3, n, width), BF16),
            vmem((3, chunks, z.nx - 1, n, LANES), BF16),
            vmem((3, chunks, n, LANES), BF16),
            vmem((2, z.reg, 2 * n, LANES), BF16),
            vmem((2, 2 * shared, LANES), BF16),
            vmem((chunks, n, LANES), BF16),
            vmem((n, width), BF16), vmem((shared, LANES), BF16), vmem((z.nx - 1, shared, LANES), BF16),
            vmem((n, width), BF16), vmem((shared, LANES), BF16), vmem((z.nx - 1, shared, LANES), BF16),
            vmem((n, width), BF16), vmem((shared, LANES), BF16), vmem((z.nx - 1, shared, LANES), BF16),
            vmem((width, n), BF16), vmem((width, n), BF16), vmem((width, n), BF16), vmem((width, n), BF16),
            vmem((2, width, z.wide), BF16), vmem((2, z.core_rows, z.wide), BF16),
            vmem((2, z.core_rows, z.wide), BF16), vmem((2, z.ny - 1, z.y_rows, z.wide), BF16),
            vmem((2, z.nzl * z.rp, z.wide), BF16), vmem((2, z.nzl, z.rp, z.wide), BF16),
            dma((3, chunks)), dma((3, chunks)),
            dma((2, chunks)), dma((2, chunks)),
            dma((3, chunks)), dma((3, chunks, z.nx - 1)),
            dma((2,)), dma((2,)), dma((2,)), dma((2, z.nx - 1)),
            dma((chunks,)), dma((chunks,)),
            dma((2, 3)), dma((2, 3)),
        ],
        compiler_params=pltpu.CompilerParams(
            collective_id=0, has_side_effects=True, vmem_limit_bytes=56 * 1024 * 1024
        ),
    )(*arrays)


def solution(mesh):
    def on_device(spatial_input, out_grad, qkv_spatial, out_spatial, qkv_temporal, out_temporal):
        width = spatial_input.shape[-1]
        tokens = spatial_input.shape[-2]
        z = Sizes(mesh.shape, tokens, width)
        cols = z.cols

        def flat(weight):
            return weight.transpose(1, 2, 0).reshape(3 * cols, width)

        grad, wt, ws = run(
            z,
            spatial_input.reshape(tokens, width), out_grad.reshape(tokens, width),
            flat(qkv_spatial), out_spatial, flat(qkv_temporal), out_temporal,
            row_order(z), row_pad(z),
        )

        def parts(w):
            return (
                w[: z.rr, : 3 * cols].reshape(z.rr, 3, cols),
                w[: z.rr, 3 * cols : 4 * cols].T,
            )

        qkv_t_grad, out_t_grad = parts(wt)
        qkv_s_grad, out_s_grad = parts(ws)
        return grad.reshape(spatial_input.shape), qkv_s_grad, out_s_grad, qkv_t_grad, out_t_grad

    placed = (
        P("dp", "sp", None, None),
        P("dp", "sp", None, None),
        P(None, None, "tp"),
        P("tp", None),
        P(None, None, "tp"),
        P("tp", None),
    )
    return jax.shard_map(
        on_device,
        mesh=mesh,
        in_specs=placed,
        out_specs=(
            P("dp", "sp", None, None),
            P(("sp", "dp"), None, "tp"),
            P("tp", ("sp", "dp")),
            P(("sp", "dp"), None, "tp"),
            P("tp", ("sp", "dp")),
        ),
        check_vma=False,
    )
```

```python
import functools

import jax
import jax.numpy as jnp
import numpy as np
from jax import lax
from jax.experimental import pallas as pl
from jax.experimental.pallas import tpu as pltpu
from jax.sharding import PartitionSpec as P

HEAD_DIM = 72
LANES = 128
ROWS = 16
MESH = pl.DeviceIdType.MESH
F32, BF16 = jnp.float32, jnp.bfloat16


def dot_nn(left, right):
    return lax.dot_general(left, right, (((1,), (0,)), ((), ())), preferred_element_type=F32)


def dot_nt(left, right):
    return lax.dot_general(left, right, (((1,), (1,)), ((), ())), preferred_element_type=F32)


def dot_tn(left, right):
    return lax.dot_general(left, right, (((0,), (0,)), ((), ())), preferred_element_type=F32)


class Sizes:
    def __init__(self, mesh_shape, tokens, width):
        self.ny, self.ns = mesh_shape["dp"], mesh_shape["sp"]
        self.nx = mesh_shape["tp"] // 2
        self.nzl = self.ns // 2
        self.tokens, self.width = tokens, width
        self.tiles = width // LANES
        self.reg = self.tiles // self.nx
        assert self.tiles == self.reg * self.nx + 1
        self.per = self.ns // self.nx
        self.cols = 2 * HEAD_DIM
        self.wide = -(-(4 * self.cols) // LANES) * LANES
        self.core_rows = width // 2
        self.y_rows = self.core_rows // self.ny
        self.rr = width // (self.ns * self.ny)
        self.packed = -(-(self.wide // LANES) * self.rr // 16) * 16


def row_order(z):
    order = np.arange(z.width).reshape(z.nzl, 2, z.ny, z.rr).transpose(1, 2, 0, 3).reshape(-1)
    onehot = np.zeros((z.width, z.width), np.float32)
    onehot[np.arange(z.width), order] = 1.0
    return onehot.astype(jnp.bfloat16)


def row_pack(z):
    tiles = z.wide // LANES
    onehot = np.zeros((z.nzl, z.packed, tiles, z.nzl, z.rr), np.float32)
    for chip in range(z.nzl):
        for tile in range(tiles):
            for row in range(z.rr):
                onehot[chip, tile * z.rr + row, tile, chip, row] = 1.0
    return onehot.reshape(z.nzl * z.packed, tiles * z.y_rows).astype(jnp.bfloat16)


def kernel(
    z,
    x_ref, ws_ref, wos_ref, go_hbm, wt_hbm, wot_hbm, order_hbm, pack_hbm,
    out_ref, wt_out, ws_out,
    go_ref, wt_ref, wot_ref, order_ref, pack_ref, load_sems,
    qkv_s, qkv_t, prob_s, prob_t, mix_s, mix_t, gm_t, grads,
    pb, rx, sb, zb, ze, eb,
    ti, tie, tig, tg, tge, tgg, got, ge, geg,
    lt_x, lt_ti, lt_go, lt_tg,
    term, term_in, yb, yr, zw, zr,
    rx_s, rx_r, zb_s, zb_r, ag_s, ag_r, go_s, go_r, gag_s, gag_r, eb_s, eb_r,
    w_s, w_r,
):
    n = z.tokens
    cols = z.cols
    factor = HEAD_DIM ** (-0.5)
    dp, s, t = lax.axis_index("dp"), lax.axis_index("sp"), lax.axis_index("tp")
    zh, xi = t // z.nx, t % z.nx
    zl, core = s // 2, s % 2
    owner = s % z.nx
    is_owner = xi == owner
    last = pl.ds((z.tiles - 1) * LANES, LANES)

    def at_x(k):
        return (dp, s, zh * z.nx + (xi + k + 1) % z.nx)

    def at_z(i):
        away, way = z.nzl - i // 4, 1 - 2 * ((i % 4) // 2)
        chip = (zh * z.nzl + zl + way * away + 2 * z.nzl) % (2 * z.nzl)
        to = (chip % z.nzl) * 2 + (core + i + 1) % 2
        return to, (dp, to, (chip // z.nzl) * z.nx + xi)

    def send(src, dst, ssem, rsem, dev):
        pltpu.make_async_remote_copy(
            src_ref=src, dst_ref=dst, send_sem=ssem, recv_sem=rsem, device_id=dev, device_id_type=MESH
        ).start()

    def wait(ref, sem):
        pltpu.make_async_copy(ref, ref, sem).wait()

    def tile_lanes(who, j, count=1):
        return pl.ds(pl.multiple_of((who * z.reg + j) * LANES, LANES), count * LANES)

    def rows_of(i, base=0):
        return pl.ds(pl.multiple_of(base + i * ROWS, ROWS), ROWS)

    loads = (
        (go_hbm, go_ref), (order_hbm, order_ref), (wt_hbm, wt_ref), (wot_hbm, wot_ref), (pack_hbm, pack_ref)
    )
    for i, (src, dst) in enumerate(loads):
        pltpu.make_async_copy(src, dst, load_sems.at[i]).start()

    def loaded(i):
        wait(loads[i][1], load_sems.at[i])

    barrier = pltpu.get_barrier_semaphore()
    for k in range(z.nx - 1):
        pl.semaphore_signal(barrier, inc=1, device_id=at_x(k), device_id_type=MESH)
    for k in range(z.ny - 1):
        pl.semaphore_signal(barrier, inc=1, device_id=((dp + k + 1) % z.ny, s, t), device_id_type=MESH)

    def greet(i, carry):
        pl.semaphore_signal(barrier, inc=1, device_id=at_z(i)[1], device_id_type=MESH)
        return carry

    lax.fori_loop(2, 2 * z.ns + 1, greet, 0)

    def send_go(i, carry):
        to = (s + i) % z.ns
        send(
            go_ref.at[rows_of(to), tile_lanes(xi, 0, z.reg)],
            got.at[rows_of(s), tile_lanes(xi, 0, z.reg)],
            go_s.at[0], go_r.at[0], (dp, to, t),
        )
        return carry

    def send_go_last(i, carry):
        to = (s + i) % z.ns
        send(go_ref.at[rows_of(to), last], ge.at[rows_of(s // z.nx)], go_s.at[1], go_r.at[1], (dp, to, t))
        return carry

    def switch_out_grad():
        pltpu.make_async_copy(
            go_ref.at[rows_of(s), tile_lanes(xi, 0, z.reg)], got.at[rows_of(s), tile_lanes(xi, 0, z.reg)], go_r.at[0]
        ).start()
        lax.fori_loop(1, z.ns, send_go, 0)

        @pl.when(is_owner)
        def _():
            pltpu.make_async_copy(go_ref.at[rows_of(s), last], ge.at[rows_of(s // z.nx)], go_r.at[1]).start()
            lax.fori_loop(1, z.ns, send_go_last, 0)

    first_head = lax.broadcasted_iota(jnp.int32, (n, cols), 1) < HEAD_DIM

    def one_head(rows, h):
        keep = first_head if h == 0 else jnp.logical_not(first_head)
        return jnp.where(keep, rows.astype(F32), 0.0).astype(BF16)

    def both_heads(pair):
        return jnp.where(first_head, pair[0], pair[1])

    def project(rows, weight_ref, qkv_ref):
        for part in range(3):
            qkv_ref[part] = dot_nt(rows, weight_ref[part * cols : (part + 1) * cols, :]).astype(BF16)

    def attend(qkv_ref, prob_ref, mix_ref, same):
        q, k, v = qkv_ref[0], qkv_ref[1], qkv_ref[2]
        mixed = []
        for h in range(2):
            scores = dot_nt(one_head(q, h), k) * factor
            if same is not None:
                scores = jnp.where(same, scores, -1e30)
            e = jnp.exp(scores - jnp.max(scores, axis=-1, keepdims=True))
            probs = e / jnp.sum(e, axis=-1, keepdims=True)
            prob_ref[h] = probs
            mixed.append(dot_nn(probs.astype(BF16), v))
        mix_ref[...] = both_heads(mixed).astype(BF16)

    def attend_back(qkv_ref, prob_ref, grad_mixed, grads_ref):
        q, k, v = qkv_ref[0], qkv_ref[1], qkv_ref[2]
        dq, dk, dv = [], [], []
        for h in range(2):
            probs = prob_ref[h]
            dp_ = dot_nt(one_head(grad_mixed, h), v)
            centre = jnp.sum(dp_ * probs, axis=-1, keepdims=True)
            ds = (probs * (dp_ - centre) * factor).astype(BF16)
            dq.append(dot_nn(ds, k))
            dk.append(dot_tn(ds, q))
            dv.append(dot_tn(probs.astype(BF16), grad_mixed))
        for part, pair in enumerate((dq, dk, dv)):
            grads_ref[part] = both_heads(pair).astype(BF16)

    def transposed(rows_ref, lt_ref):
        step = 192 if z.width % 192 == 0 else 160

        def one(i, carry):
            at = pl.ds(pl.multiple_of(i * step, 16), step)
            lt_ref[at, :] = dot_nt(order_ref[at, :], rows_ref[...]).astype(BF16)
            return carry

        lax.fori_loop(0, z.width // step, one, 0)

    def send_x(p, j):
        for k in range(z.nx - 1):
            to = (xi + k + 1) % z.nx
            send(pb.at[p, :, tile_lanes(to, j)], rx.at[p, j, k], rx_s.at[p, j], rx_r.at[p, j], at_x(k))

    def send_x_last(p):
        @pl.when(jnp.logical_not(is_owner))
        def _():
            k = (owner - xi - 1 + z.nx) % z.nx
            send(
                pb.at[p, :, last], rx.at[p, z.reg, k], rx_s.at[p, z.reg], rx_r.at[p, z.reg],
                (dp, s, zh * z.nx + owner),
            )

    def partial_and_send(p, product):
        for j in range(z.reg):
            for who in range(z.nx):
                lanes = slice((who * z.reg + j) * LANES, (who * z.reg + j + 1) * LANES)
                pb[p, :, lanes] = product(lanes).astype(BF16)
            send_x(p, j)
        lanes = slice((z.tiles - 1) * LANES, z.tiles * LANES)
        pb[p, :, lanes] = product(lanes).astype(BF16)
        send_x_last(p)

    def sum_x(p, j, extra=None):
        wait(rx.at[p, j], rx_r.at[p, j])
        lanes = tile_lanes(xi, j) if j < z.reg else last
        total = pb[p, :, lanes].astype(F32)
        for k in range(z.nx - 1):
            total += rx[p, j, k].astype(F32)
        if extra is not None:
            total += extra(lanes)
        sb[p, j] = total.astype(BF16)

    def send_z(p, j):
        if j < z.reg:
            pltpu.make_async_copy(sb.at[p, j, rows_of(s)], zb.at[p, j, rows_of(s, zh * n)], zb_r.at[p, j]).start()
        else:
            pltpu.make_async_copy(
                sb.at[p, j, rows_of(s)], ze.at[p, rows_of(s // z.nx, zh * z.per * ROWS)], zb_r.at[p, j]
            ).start()

        def one(i, carry):
            to, dev = at_z(i)
            dst = zb.at[p, j, rows_of(s, zh * n)] if j < z.reg else ze.at[p, rows_of(s // z.nx, zh * z.per * ROWS)]
            send(sb.at[p, j, rows_of(to)], dst, zb_s.at[p, j], zb_r.at[p, j], dev)
            return carry

        lax.fori_loop(2, 2 * z.ns + 1, one, 0)

    def switch(p, extra=None):
        for j in range(z.reg):
            sum_x(p, j, extra)
            send_z(p, j)

        @pl.when(is_owner)
        def _():
            sum_x(p, z.reg, extra)
            send_z(p, z.reg)

    def sum_z(p, full, mine, others, extra=None):
        for j in range(z.reg):
            wait(zb.at[p, j], zb_r.at[p, j])
            lanes = tile_lanes(xi, j)
            total = zb[p, j, 0:n].astype(F32) + zb[p, j, n : 2 * n].astype(F32)
            if extra is not None:
                total += extra[:, lanes].astype(F32)
            full[:, lanes] = total.astype(BF16)
            for k in range(z.nx - 1):
                send(full.at[:, lanes], full.at[:, lanes], ag_s.at[p, j], ag_r.at[p, j, k], at_x(k))
        wait(ze.at[p], zb_r.at[p, z.reg])
        half = z.per * ROWS
        for i in range(z.per):
            total = ze[p, i * ROWS : (i + 1) * ROWS].astype(F32)
            total += ze[p, half + i * ROWS : half + (i + 1) * ROWS].astype(F32)
            if extra is not None:
                total += extra[rows_of(xi + z.nx * i), last].astype(F32)
            mine[i * ROWS : (i + 1) * ROWS, :] = total.astype(BF16)
        for k in range(z.nx - 1):
            send(mine, others.at[k], ag_s.at[p, z.reg], ag_r.at[p, z.reg, k], at_x(k))

    def place_last(full, block, who):
        for i in range(z.per):
            full[rows_of(who + z.nx * i), last] = block[i * ROWS : (i + 1) * ROWS, :]

    def gather_x(p, full, mine, others):
        place_last(full, mine, xi)
        for k in range(z.nx - 1):
            who = (xi - k - 1 + z.nx) % z.nx
            for j in range(z.reg):
                wait(full.at[:, tile_lanes(who, j)], ag_r.at[p, j, k])
            wait(others.at[k], ag_r.at[p, z.reg, k])
            place_last(full, others.at[k], who)

    def weight_terms(b, lt_qkv, lt_out, mix_ref):
        tail = z.wide - LANES * (3 * cols // LANES)
        base = z.wide - tail
        packed = jnp.concatenate(
            [grads[b, 0], grads[b, 1], grads[b, 2], jnp.zeros((n, z.wide - 3 * cols), BF16)], axis=1
        )
        placed = jnp.concatenate(
            [jnp.zeros((n, 3 * cols - base), BF16), mix_ref[...], jnp.zeros((n, z.wide - 4 * cols), BF16)], axis=1
        )
        step = 192 if z.width % 192 == 0 else 160

        def one(i, carry):
            at = pl.ds(pl.multiple_of(i * step, 16), step)
            left, left_out = lt_qkv[at, :], lt_out[at, :]
            term[b, at, 0:base] = dot_nn(left, packed[:, 0:base]).astype(BF16)
            term[b, at, base : z.wide] = (dot_nn(left, packed[:, base:]) + dot_nn(left_out, placed)).astype(BF16)
            return carry

        lax.fori_loop(0, z.width // step, one, 0)
        away = pl.ds(pl.multiple_of((1 - core) * z.core_rows, 16), z.core_rows)
        send(term.at[b, away], term_in.at[b], w_s.at[b, 0], w_r.at[b, 0], (dp, s + 1 - 2 * core, t))

    def weights_y(b):
        wait(term_in.at[b], w_r.at[b, 0])
        here = pl.ds(pl.multiple_of(core * z.core_rows, 16), z.core_rows)
        yb[b] = (term[b, here].astype(F32) + term_in[b].astype(F32)).astype(BF16)
        for k in range(z.ny - 1):
            to = (dp + k + 1) % z.ny
            src = yb.at[b, pl.ds(pl.multiple_of(to * z.y_rows, 16), z.y_rows)]
            send(src, yr.at[b, k], w_s.at[b, 1], w_r.at[b, 1], (to, s, t))

    def weights_z(b):
        wait(yr.at[b], w_r.at[b, 1])
        total = yb[b, pl.ds(pl.multiple_of(dp * z.y_rows, 16), z.y_rows)].astype(F32)
        for k in range(z.ny - 1):
            total += yr[b, k].astype(F32)
        total = total.astype(BF16)
        stacked = jnp.concatenate([total[:, i : i + LANES] for i in range(0, z.wide, LANES)], axis=0)
        zw[b] = dot_nn(pack_ref[...], stacked).astype(BF16)

        def block(i):
            return pl.ds(pl.multiple_of(i * z.packed, 16), z.packed)

        pltpu.make_async_copy(zw.at[b, block(zl)], zr.at[b, zl], w_r.at[b, 2]).start()
        for k in range(z.nzl - 1):
            to = (zl + k + 1) % z.nzl
            send(zw.at[b, block(to)], zr.at[b, zl], w_s.at[b, 2], w_r.at[b, 2], (dp, 2 * to + core, t))

    def weights_end(b, w_out):
        wait(zr.at[b], w_r.at[b, 2])
        total = zr[b, 0].astype(F32)
        for k in range(1, z.nzl):
            total += zr[b, k].astype(F32)
        w_out[...] = total

    project(x_ref[...], ws_ref, qkv_s)
    attend(qkv_s, prob_s, mix_s, None)
    pl.semaphore_wait(barrier, (z.nx - 1) + (z.ny - 1) + (2 * z.ns - 1))
    partial_and_send(0, lambda lanes: dot_nn(mix_s[...], wos_ref[:, lanes]))
    loaded(0)
    switch_out_grad()

    def add_input(lanes):
        return x_ref[:, lanes].astype(F32) * jnp.where(zh == 0, 1.0, 0.0)

    switch(0, add_input)

    wait(got.at[:, tile_lanes(xi, 0, z.reg)], go_r.at[0])
    wait(ge, go_r.at[1])
    for k in range(z.nx - 1):
        lanes = tile_lanes(xi, 0, z.reg)
        send(got.at[:, lanes], got.at[:, lanes], gag_s.at[0], gag_r.at[0, k], at_x(k))
        send(ge, geg.at[k], gag_s.at[1], gag_r.at[1, k], at_x(k))
    loaded(1)
    transposed(x_ref, lt_x)

    sum_z(0, ti, tie, tig)

    place_last(got, ge, xi)
    for k in range(z.nx - 1):
        who = (xi - k - 1 + z.nx) % z.nx
        wait(got.at[:, tile_lanes(who, 0, z.reg)], gag_r.at[0, k])
        wait(geg.at[k], gag_r.at[1, k])
        place_last(got, geg.at[k], who)
    loaded(2)
    loaded(3)
    gm_t[...] = dot_nt(got[...], wot_ref[...]).astype(BF16)
    transposed(got, lt_go)
    gather_x(0, ti, tie, tig)

    rows_i = lax.broadcasted_iota(jnp.int32, (n, n), 0)
    cols_i = lax.broadcasted_iota(jnp.int32, (n, n), 1)
    same = (rows_i & (ROWS - 1)) == (cols_i & (ROWS - 1))
    project(ti[...], wt_ref, qkv_t)
    attend(qkv_t, prob_t, mix_t, same)
    attend_back(qkv_t, prob_t, gm_t[...], grads.at[0])

    def back(b, weight_ref):
        def product(lanes):
            total = dot_nn(grads[b, 0], weight_ref[0:cols, lanes])
            for part in range(1, 3):
                total += dot_nn(grads[b, part], weight_ref[part * cols : (part + 1) * cols, lanes])
            return total

        return product

    partial_and_send(1, back(0, wt_ref))
    transposed(ti, lt_ti)
    weight_terms(0, lt_ti, lt_go, mix_t)
    switch(1)
    weights_y(0)
    sum_z(1, tg, tge, tgg, go_ref)
    loaded(4)
    weights_z(0)
    gather_x(1, tg, tge, tgg)

    grad_mixed_s = dot_nt(tg[...], wos_ref[...]).astype(BF16)
    attend_back(qkv_s, prob_s, grad_mixed_s, grads.at[1])
    partial_and_send(2, back(1, ws_ref))
    transposed(tg, lt_tg)
    weight_terms(1, lt_x, lt_tg, mix_s)

    def exchange(j):
        sum_x(2, j)
        send(sb.at[2, j], eb.at[j], eb_s.at[j], eb_r.at[j], (dp, s, (1 - zh) * z.nx + xi))

    def finish(j, k_sem):
        wait(eb.at[j], eb_r.at[j])
        lanes = tile_lanes(xi, j) if j < z.reg else last
        total = tg[:, lanes].astype(F32) + (sb[2, j].astype(F32) + eb[j].astype(F32))
        out_ref[:, lanes] = total.astype(BF16)
        for k in range(z.nx - 1):
            send(out_ref.at[:, lanes], out_ref.at[:, lanes], ag_s.at[2, j], ag_r.at[2, j, k_sem(k)], at_x(k))

    for j in range(z.reg):
        exchange(j)

    @pl.when(is_owner)
    def _():
        exchange(z.reg)

    weights_y(1)
    weights_z(1)
    for j in range(z.reg):
        finish(j, lambda k: k)

    @pl.when(is_owner)
    def _():
        finish(z.reg, lambda k: 0)

    weights_end(0, wt_out)
    for k in range(z.nx - 1):
        who = (xi - k - 1 + z.nx) % z.nx
        for j in range(z.reg):
            wait(out_ref.at[:, tile_lanes(who, j)], ag_r.at[2, j, k])

    @pl.when(jnp.logical_not(is_owner))
    def _():
        wait(out_ref.at[:, last], ag_r.at[2, z.reg, 0])

    weights_end(1, ws_out)

    for p in range(3):
        for j in range(z.reg):
            wait(rx.at[p, j], rx_s.at[p, j])
            wait(rx.at[p, j], ag_s.at[p, j])

        @pl.when(jnp.logical_not(is_owner))
        def _():
            wait(rx.at[p, z.reg, 0], rx_s.at[p, z.reg])

    sent = (2 * z.ns - 1) * ROWS
    for p in range(2):
        for j in range(z.reg):
            wait(zb.at[p, j, pl.ds(0, sent)], zb_s.at[p, j])
        wait(tig if p == 0 else tgg, ag_s.at[p, z.reg])

        @pl.when(is_owner)
        def _():
            wait(zb.at[p, 0, pl.ds(0, sent)], zb_s.at[p, z.reg])

    for j in range(z.reg):
        wait(eb.at[j], eb_s.at[j])

    @pl.when(is_owner)
    def _():
        wait(eb.at[z.reg], eb_s.at[z.reg])
        wait(rx.at[2, z.reg], ag_s.at[2, z.reg])
        wait(got.at[pl.ds(0, (z.ns - 1) * ROWS), last], go_s.at[1])

    wait(got.at[pl.ds(0, (z.ns - 1) * ROWS), pl.ds(0, z.reg * LANES)], go_s.at[0])
    wait(got.at[:, pl.ds(0, (z.nx - 1) * z.reg * LANES)], gag_s.at[0])
    wait(geg, gag_s.at[1])
    for b in range(2):
        wait(term_in.at[b], w_s.at[b, 0])
        wait(yr.at[b], w_s.at[b, 1])
        wait(zr.at[b, pl.ds(0, z.nzl - 1)], w_s.at[b, 2])


def finish_kernel(z, grad_ref, wt_ref, ws_ref, grad_out, qkv_s_out, out_s_out, qkv_t_out, out_t_out, sem):
    copy = pltpu.make_async_copy(grad_ref, grad_out, sem)
    copy.start()
    for w_ref, qkv_out, out_out in ((ws_ref, qkv_s_out, out_s_out), (wt_ref, qkv_t_out, out_t_out)):
        rows = [w_ref[i * z.rr : (i + 1) * z.rr, :] for i in range(z.wide // LANES)]
        rows = jnp.concatenate(rows, axis=1)
        for part in range(3):
            qkv_out[:, part, :] = rows[:, part * z.cols : (part + 1) * z.cols]
        out_out[...] = rows[:, 3 * z.cols : 4 * z.cols]
    copy.wait()


def finish(z, *arrays):
    hbm, vmem = pl.BlockSpec(memory_space=pltpu.HBM), pl.BlockSpec(memory_space=pltpu.VMEM)
    qkv = jax.ShapeDtypeStruct((z.rr, 3, z.cols), F32)
    out = jax.ShapeDtypeStruct((z.rr, z.cols), F32)
    return pl.pallas_call(
        functools.partial(finish_kernel, z),
        out_shape=(jax.ShapeDtypeStruct((z.tokens, z.width), BF16), qkv, out, qkv, out),
        in_specs=[hbm, vmem, vmem],
        out_specs=[hbm] + [vmem] * 4,
        scratch_shapes=[pltpu.SemaphoreType.DMA],
    )(*arrays)


def run(z, *arrays):
    n, width, cols = z.tokens, z.width, z.cols
    chunks = z.reg + 1
    dma = pltpu.SemaphoreType.DMA
    vmem = pltpu.VMEM
    shared = z.per * ROWS
    return pl.pallas_call(
        functools.partial(kernel, z),
        out_shape=(
            jax.ShapeDtypeStruct((n, width), BF16),
            jax.ShapeDtypeStruct((z.packed, LANES), F32),
            jax.ShapeDtypeStruct((z.packed, LANES), F32),
        ),
        in_specs=[pl.BlockSpec(memory_space=pltpu.VMEM)] * 3 + [pl.BlockSpec(memory_space=pl.ANY)] * 5,
        out_specs=[pl.BlockSpec(memory_space=pltpu.VMEM)] * 3,
        scratch_shapes=[
            vmem((n, width), BF16), vmem((3 * cols, width), BF16), vmem((cols, width), BF16),
            vmem((width, width), BF16), vmem((z.nzl * z.packed, z.wide // LANES * z.y_rows), BF16), dma((5,)),
            vmem((3, n, cols), BF16), vmem((3, n, cols), BF16),
            vmem((2, n, n), F32), vmem((2, n, n), F32),
            vmem((n, cols), BF16), vmem((n, cols), BF16), vmem((n, cols), BF16),
            vmem((2, 3, n, cols), BF16),
            vmem((3, n, width), BF16),
            vmem((3, chunks, z.nx - 1, n, LANES), BF16),
            vmem((3, chunks, n, LANES), BF16),
            vmem((2, z.reg, 2 * n, LANES), BF16),
            vmem((2, 2 * shared, LANES), BF16),
            vmem((chunks, n, LANES), BF16),
            vmem((n, width), BF16), vmem((shared, LANES), BF16), vmem((z.nx - 1, shared, LANES), BF16),
            vmem((n, width), BF16), vmem((shared, LANES), BF16), vmem((z.nx - 1, shared, LANES), BF16),
            vmem((n, width), BF16), vmem((shared, LANES), BF16), vmem((z.nx - 1, shared, LANES), BF16),
            vmem((width, n), BF16), vmem((width, n), BF16), vmem((width, n), BF16), vmem((width, n), BF16),
            vmem((2, width, z.wide), BF16), vmem((2, z.core_rows, z.wide), BF16),
            vmem((2, z.core_rows, z.wide), BF16), vmem((2, z.ny - 1, z.y_rows, z.wide), BF16),
            vmem((2, z.nzl * z.packed, LANES), BF16), vmem((2, z.nzl, z.packed, LANES), BF16),
            dma((3, chunks)), dma((3, chunks)),
            dma((2, chunks)), dma((2, chunks)),
            dma((3, chunks)), dma((3, chunks, z.nx - 1)),
            dma((2,)), dma((2,)), dma((2,)), dma((2, z.nx - 1)),
            dma((chunks,)), dma((chunks,)),
            dma((2, 3)), dma((2, 3)),
        ],
        compiler_params=pltpu.CompilerParams(
            collective_id=0, has_side_effects=True, vmem_limit_bytes=56 * 1024 * 1024
        ),
    )(*arrays)


def solution(mesh):
    def on_device(spatial_input, out_grad, qkv_spatial, out_spatial, qkv_temporal, out_temporal):
        width = spatial_input.shape[-1]
        tokens = spatial_input.shape[-2]
        z = Sizes(mesh.shape, tokens, width)
        cols = z.cols

        def flat(weight):
            return weight.transpose(1, 2, 0).reshape(3 * cols, width)

        grad, wt, ws = run(
            z,
            spatial_input.reshape(tokens, width), flat(qkv_spatial), out_spatial,
            out_grad.reshape(tokens, width), flat(qkv_temporal), out_temporal,
            row_order(z), row_pack(z),
        )
        grad, qkv_s_grad, out_s_grad, qkv_t_grad, out_t_grad = finish(z, grad, wt, ws)
        return grad.reshape(spatial_input.shape), qkv_s_grad, out_s_grad.T, qkv_t_grad, out_t_grad.T

    placed = (
        P("dp", "sp", None, None),
        P("dp", "sp", None, None),
        P(None, None, "tp"),
        P("tp", None),
        P(None, None, "tp"),
        P("tp", None),
    )
    return jax.shard_map(
        on_device,
        mesh=mesh,
        in_specs=placed,
        out_specs=(
            P("dp", "sp", None, None),
            P(("sp", "dp"), None, "tp"),
            P("tp", ("sp", "dp")),
            P(("sp", "dp"), None, "tp"),
            P("tp", ("sp", "dp")),
        ),
        check_vma=False,
    )
```

```python
import functools

import jax
import jax.numpy as jnp
import numpy as np
from jax import lax
from jax.experimental import pallas as pl
from jax.experimental.pallas import tpu as pltpu
from jax.sharding import PartitionSpec as P

HEAD_DIM = 72
LANES = 128
ROWS = 16
MESH = pl.DeviceIdType.MESH
F32, BF16 = jnp.float32, jnp.bfloat16


def dot_nn(left, right):
    return lax.dot_general(left, right, (((1,), (0,)), ((), ())), preferred_element_type=F32)


def dot_nt(left, right):
    return lax.dot_general(left, right, (((1,), (1,)), ((), ())), preferred_element_type=F32)


def dot_tn(left, right):
    return lax.dot_general(left, right, (((0,), (0,)), ((), ())), preferred_element_type=F32)


class Sizes:
    def __init__(self, mesh_shape, tokens, width):
        self.ny, self.ns = mesh_shape["dp"], mesh_shape["sp"]
        self.nx = mesh_shape["tp"] // 2
        self.nzl = self.ns // 2
        self.tokens, self.width = tokens, width
        self.tiles = width // LANES
        self.reg = self.tiles // self.nx
        assert self.tiles == self.reg * self.nx + 1
        self.per = self.ns // self.nx
        self.cols = 2 * HEAD_DIM
        self.wide = -(-(4 * self.cols) // LANES) * LANES
        self.core_rows = width // 2
        self.y_rows = self.core_rows // self.ny
        self.rr = width // (self.ns * self.ny)
        self.packed = -(-(self.wide // LANES) * self.rr // 16) * 16


def row_order(z):
    order = np.arange(z.width).reshape(z.nzl, 2, z.ny, z.rr).transpose(1, 2, 0, 3).reshape(-1)
    onehot = np.zeros((z.width, z.width), np.float32)
    onehot[np.arange(z.width), order] = 1.0
    return onehot.astype(jnp.bfloat16)


def row_pack(z):
    tiles = z.wide // LANES
    onehot = np.zeros((z.nzl, z.packed, tiles, z.nzl, z.rr), np.float32)
    for chip in range(z.nzl):
        for tile in range(tiles):
            for row in range(z.rr):
                onehot[chip, tile * z.rr + row, tile, chip, row] = 1.0
    return onehot.reshape(z.nzl * z.packed, tiles * z.y_rows).astype(jnp.bfloat16)


def kernel(
    z,
    x_hbm, ws_hbm, wos_hbm, go_hbm, wt_hbm, wot_hbm, order_hbm, pack_hbm,
    out_ref, wt_out, ws_out,
    x_ref, ws_ref, wos_ref, go_ref, wt_ref, wot_ref, order_ref, pack_ref, load_sems,
    qkv_s, qkv_t, prob_s, prob_t, mix_s, mix_t, mix_ts, gm_s, gm_t, grads,
    pb, rx, sb, zb, ze, eb,
    ti, tie, tig, tg, tge, tgg,
    lt_x, lt_ti, lt_go, lt_tg,
    term, term_in, yb, yr, zw, zr,
    rx_s, rx_r, zb_s, zb_r, ag_s, ag_r, hd_s, hd_r, eb_s, eb_r,
    w_s, w_r,
):
    n = z.tokens
    cols = z.cols
    factor = HEAD_DIM ** (-0.5)
    dp, s, t = lax.axis_index("dp"), lax.axis_index("sp"), lax.axis_index("tp")
    zh, xi = t // z.nx, t % z.nx
    zl, core = s // 2, s % 2
    owner = s % z.nx
    is_owner = xi == owner
    last = pl.ds((z.tiles - 1) * LANES, LANES)

    def at_x(k):
        return (dp, s, zh * z.nx + (xi + k + 1) % z.nx)

    def at_z(i):
        away, way = z.nzl - i // 4, 1 - 2 * ((i % 4) // 2)
        chip = (zh * z.nzl + zl + way * away + 2 * z.nzl) % (2 * z.nzl)
        to = (chip % z.nzl) * 2 + (core + i + 1) % 2
        return to, (dp, to, (chip // z.nzl) * z.nx + xi)

    def send(src, dst, ssem, rsem, dev):
        pltpu.make_async_remote_copy(
            src_ref=src, dst_ref=dst, send_sem=ssem, recv_sem=rsem, device_id=dev, device_id_type=MESH
        ).start()

    def wait(ref, sem):
        pltpu.make_async_copy(ref, ref, sem).wait()

    leaving = []

    def on_leaving():
        for ref, place, sem, sem_place, of_owner in leaving:
            def gone():
                wait(ref.at[place] if place else ref, sem.at[sem_place])

            if of_owner is None:
                gone()
            else:
                pl.when(is_owner if of_owner else jnp.logical_not(is_owner))(gone)

    sent_z = pl.ds(0, (2 * z.ns - 1) * ROWS)
    sent_sp = pl.ds(0, (z.ns - 1) * ROWS)

    def tile_lanes(who, j, count=1):
        return pl.ds(pl.multiple_of((who * z.reg + j) * LANES, LANES), count * LANES)

    def rows_of(i, base=0):
        return pl.ds(pl.multiple_of(base + i * ROWS, ROWS), ROWS)

    barrier = pltpu.get_barrier_semaphore()
    def greet(i, carry):
        pl.semaphore_signal(barrier, inc=1, device_id=at_z(i)[1], device_id_type=MESH)
        return carry

    lax.fori_loop(2, 2 * z.ns + 1, greet, 0)
    for k in range(z.nx - 1):
        pl.semaphore_signal(barrier, inc=1, device_id=at_x(k), device_id_type=MESH)
    for k in range(z.ny - 1):
        pl.semaphore_signal(barrier, inc=1, device_id=((dp + k + 1) % z.ny, s, t), device_id_type=MESH)

    loads = (
        (x_hbm, x_ref), (ws_hbm, ws_ref), (wos_hbm, wos_ref), (wot_hbm, wot_ref), (go_hbm, go_ref),
        (order_hbm, order_ref), (wt_hbm, wt_ref), (pack_hbm, pack_ref),
    )
    for i, (src, dst) in enumerate(loads):
        pltpu.make_async_copy(src, dst, load_sems.at[i]).start()

    def loaded(*which):
        for i in which:
            wait(loads[i][1], load_sems.at[i])

    def switch_heads(b, src, dst):
        pltpu.make_async_copy(src.at[rows_of(s)], dst.at[rows_of(s)], hd_r.at[b]).start()

        def one(i, carry):
            to = (s + i) % z.ns
            send(src.at[rows_of(to)], dst.at[rows_of(s)], hd_s.at[b], hd_r.at[b], (dp, to, t))
            return carry

        lax.fori_loop(1, z.ns, one, 0)
        leaving.append((dst, (sent_sp,), hd_s, (b,), None))

    first_head = lax.broadcasted_iota(jnp.int32, (n, cols), 1) < HEAD_DIM

    def one_head(rows, h):
        keep = first_head if h == 0 else jnp.logical_not(first_head)
        return jnp.where(keep, rows.astype(F32), 0.0).astype(BF16)

    def both_heads(pair):
        return jnp.where(first_head, pair[0], pair[1])

    def project(rows, weight_ref, qkv_ref):
        for part in range(3):
            qkv_ref[part] = dot_nt(rows, weight_ref[part * cols : (part + 1) * cols, :]).astype(BF16)

    def attend(qkv_ref, prob_ref, mix_ref, same):
        q, k, v = qkv_ref[0], qkv_ref[1], qkv_ref[2]
        mixed = []
        for h in range(2):
            scores = dot_nt(one_head(q, h), k) * factor
            if same is not None:
                scores = jnp.where(same, scores, -1e30)
            e = jnp.exp(scores - jnp.max(scores, axis=-1, keepdims=True))
            probs = e / jnp.sum(e, axis=-1, keepdims=True)
            prob_ref[h] = probs
            mixed.append(dot_nn(probs.astype(BF16), v))
        mix_ref[...] = both_heads(mixed).astype(BF16)

    def attend_back(qkv_ref, prob_ref, grad_mixed, grads_ref):
        q, k, v = qkv_ref[0], qkv_ref[1], qkv_ref[2]
        dq, dk, dv = [], [], []
        for h in range(2):
            probs = prob_ref[h]
            dp_ = dot_nt(one_head(grad_mixed, h), v)
            centre = jnp.sum(dp_ * probs, axis=-1, keepdims=True)
            ds = (probs * (dp_ - centre) * factor).astype(BF16)
            dq.append(dot_nn(ds, k))
            dk.append(dot_tn(ds, q))
            dv.append(dot_tn(probs.astype(BF16), grad_mixed))
        for part, pair in enumerate((dq, dk, dv)):
            grads_ref[part] = both_heads(pair).astype(BF16)

    def transposed(rows_ref, lt_ref):
        step = 192 if z.width % 192 == 0 else 160

        def one(i, carry):
            at = pl.ds(pl.multiple_of(i * step, 16), step)
            lt_ref[at, :] = dot_nt(order_ref[at, :], rows_ref[...]).astype(BF16)
            return carry

        lax.fori_loop(0, z.width // step, one, 0)

    def send_x(p, j):
        for k in range(z.nx - 1):
            to = (xi + k + 1) % z.nx
            send(pb.at[p, :, tile_lanes(to, j)], rx.at[p, j, k], rx_s.at[p, j], rx_r.at[p, j], at_x(k))
        leaving.append((rx, (p, j,), rx_s, (p, j,), None))

    def send_x_last(p):
        leaving.append((rx, (p, z.reg, 0,), rx_s, (p, z.reg,), False))

        @pl.when(jnp.logical_not(is_owner))
        def _():
            k = (owner - xi - 1 + z.nx) % z.nx
            send(
                pb.at[p, :, last], rx.at[p, z.reg, k], rx_s.at[p, z.reg], rx_r.at[p, z.reg],
                (dp, s, zh * z.nx + owner),
            )

    def partial_and_send(p, product):
        for j in range(z.reg):
            for who in range(z.nx):
                lanes = slice((who * z.reg + j) * LANES, (who * z.reg + j + 1) * LANES)
                pb[p, :, lanes] = product(lanes).astype(BF16)
            send_x(p, j)
        lanes = slice((z.tiles - 1) * LANES, z.tiles * LANES)
        pb[p, :, lanes] = product(lanes).astype(BF16)
        send_x_last(p)

    def sum_x(p, j, extra=None):
        wait(rx.at[p, j], rx_r.at[p, j])
        lanes = tile_lanes(xi, j) if j < z.reg else last
        total = pb[p, :, lanes].astype(F32)
        for k in range(z.nx - 1):
            total += rx[p, j, k].astype(F32)
        if extra is not None:
            total += extra(lanes)
        sb[p, j] = total.astype(BF16)

    def send_z(p, j):
        if j < z.reg:
            pltpu.make_async_copy(sb.at[p, j, rows_of(s)], zb.at[p, j, rows_of(s, zh * n)], zb_r.at[p, j]).start()
        else:
            pltpu.make_async_copy(
                sb.at[p, j, rows_of(s)], ze.at[p, rows_of(s // z.nx, zh * z.per * ROWS)], zb_r.at[p, j]
            ).start()

        def one(i, carry):
            to, dev = at_z(i)
            dst = zb.at[p, j, rows_of(s, zh * n)] if j < z.reg else ze.at[p, rows_of(s // z.nx, zh * z.per * ROWS)]
            send(sb.at[p, j, rows_of(to)], dst, zb_s.at[p, j], zb_r.at[p, j], dev)
            return carry

        lax.fori_loop(2, 2 * z.ns + 1, one, 0)
        leaving.append((zb, (p, 0, sent_z,), zb_s, (p, j,), None if j < z.reg else True))

    def switch(p, extra=None):
        for j in range(z.reg):
            sum_x(p, j, extra)
            send_z(p, j)

        @pl.when(is_owner)
        def _():
            sum_x(p, z.reg, extra)
            send_z(p, z.reg)

    def sum_z(p, full, mine, others, extra=None):
        for j in range(z.reg):
            wait(zb.at[p, j], zb_r.at[p, j])
            lanes = tile_lanes(xi, j)
            total = zb[p, j, 0:n].astype(F32) + zb[p, j, n : 2 * n].astype(F32)
            if extra is not None:
                total += extra[:, lanes].astype(F32)
            full[:, lanes] = total.astype(BF16)
            for k in range(z.nx - 1):
                send(full.at[:, lanes], full.at[:, lanes], ag_s.at[p, j], ag_r.at[p, j, k], at_x(k))
            leaving.append((rx, (p, j,), ag_s, (p, j,), None))
        wait(ze.at[p], zb_r.at[p, z.reg])
        half = z.per * ROWS
        for i in range(z.per):
            total = ze[p, i * ROWS : (i + 1) * ROWS].astype(F32)
            total += ze[p, half + i * ROWS : half + (i + 1) * ROWS].astype(F32)
            if extra is not None:
                total += extra[rows_of(xi + z.nx * i), last].astype(F32)
            mine[i * ROWS : (i + 1) * ROWS, :] = total.astype(BF16)
        for k in range(z.nx - 1):
            send(mine, others.at[k], ag_s.at[p, z.reg], ag_r.at[p, z.reg, k], at_x(k))
        leaving.append((others, (), ag_s, (p, z.reg,), None))

    def place_last(full, block, who):
        for i in range(z.per):
            full[rows_of(who + z.nx * i), last] = block[i * ROWS : (i + 1) * ROWS, :]

    def gather_x(p, full, mine, others):
        place_last(full, mine, xi)
        for k in range(z.nx - 1):
            who = (xi - k - 1 + z.nx) % z.nx
            for j in range(z.reg):
                wait(full.at[:, tile_lanes(who, j)], ag_r.at[p, j, k])
            wait(others.at[k], ag_r.at[p, z.reg, k])
            place_last(full, others.at[k], who)

    def weight_terms(b, lt_qkv, lt_out, mix_ref):
        tail = z.wide - LANES * (3 * cols // LANES)
        base = z.wide - tail
        packed = jnp.concatenate(
            [grads[b, 0], grads[b, 1], grads[b, 2], jnp.zeros((n, z.wide - 3 * cols), BF16)], axis=1
        )
        placed = jnp.concatenate(
            [jnp.zeros((n, 3 * cols - base), BF16), mix_ref[...], jnp.zeros((n, z.wide - 4 * cols), BF16)], axis=1
        )
        step = 192 if z.width % 192 == 0 else 160

        def one(i, carry):
            at = pl.ds(pl.multiple_of(i * step, 16), step)
            left, left_out = lt_qkv[at, :], lt_out[at, :]
            term[b, at, 0:base] = dot_nn(left, packed[:, 0:base]).astype(BF16)
            term[b, at, base : z.wide] = (dot_nn(left, packed[:, base:]) + dot_nn(left_out, placed)).astype(BF16)
            return carry

        lax.fori_loop(0, z.width // step, one, 0)
        away = pl.ds(pl.multiple_of((1 - core) * z.core_rows, 16), z.core_rows)
        send(term.at[b, away], term_in.at[b], w_s.at[b, 0], w_r.at[b, 0], (dp, s + 1 - 2 * core, t))
        leaving.append((term_in, (b,), w_s, (b, 0,), None))

    def weights_y(b):
        wait(term_in.at[b], w_r.at[b, 0])
        here = pl.ds(pl.multiple_of(core * z.core_rows, 16), z.core_rows)
        yb[b] = (term[b, here].astype(F32) + term_in[b].astype(F32)).astype(BF16)
        for k in range(z.ny - 1):
            to = (dp + k + 1) % z.ny
            src = yb.at[b, pl.ds(pl.multiple_of(to * z.y_rows, 16), z.y_rows)]
            send(src, yr.at[b, k], w_s.at[b, 1], w_r.at[b, 1], (to, s, t))
        leaving.append((yr, (b,), w_s, (b, 1,), None))

    def weights_z(b):
        wait(yr.at[b], w_r.at[b, 1])
        total = yb[b, pl.ds(pl.multiple_of(dp * z.y_rows, 16), z.y_rows)].astype(F32)
        for k in range(z.ny - 1):
            total += yr[b, k].astype(F32)
        total = total.astype(BF16)
        stacked = jnp.concatenate([total[:, i : i + LANES] for i in range(0, z.wide, LANES)], axis=0)
        zw[b] = dot_nn(pack_ref[...], stacked).astype(BF16)

        def block(i):
            return pl.ds(pl.multiple_of(i * z.packed, 16), z.packed)

        pltpu.make_async_copy(zw.at[b, block(zl)], zr.at[b, zl], w_r.at[b, 2]).start()
        for k in range(z.nzl - 1):
            to = (zl + k + 1) % z.nzl
            send(zw.at[b, block(to)], zr.at[b, zl], w_s.at[b, 2], w_r.at[b, 2], (dp, 2 * to + core, t))
        leaving.append((zr, (b, pl.ds(0, z.nzl - 1),), w_s, (b, 2,), None))

    def weights_end(b, w_out):
        wait(zr.at[b], w_r.at[b, 2])
        total = zr[b, 0].astype(F32)
        for k in range(1, z.nzl):
            total += zr[b, k].astype(F32)
        w_out[...] = total

    loaded(0, 1)
    project(x_ref[...], ws_ref, qkv_s)
    attend(qkv_s, prob_s, mix_s, None)
    loaded(2)
    pl.semaphore_wait(barrier, (z.nx - 1) + (z.ny - 1) + (2 * z.ns - 1))
    partial_and_send(0, lambda lanes: dot_nn(mix_s[...], wos_ref[:, lanes]))
    loaded(3, 4)
    gm_s[...] = dot_nt(go_ref[...], wot_ref[...]).astype(BF16)

    def add_input(lanes):
        return x_ref[:, lanes].astype(F32) * jnp.where(zh == 0, 1.0, 0.0)

    switch(0, add_input)
    switch_heads(0, gm_s, gm_t)
    loaded(5)
    transposed(x_ref, lt_x)
    transposed(go_ref, lt_go)
    sum_z(0, ti, tie, tig)
    loaded(6)
    gather_x(0, ti, tie, tig)

    rows_i = lax.broadcasted_iota(jnp.int32, (n, n), 0)
    cols_i = lax.broadcasted_iota(jnp.int32, (n, n), 1)
    same = (rows_i & (ROWS - 1)) == (cols_i & (ROWS - 1))
    project(ti[...], wt_ref, qkv_t)
    attend(qkv_t, prob_t, mix_t, same)
    switch_heads(1, mix_t, mix_ts)
    wait(gm_t, hd_r.at[0])
    attend_back(qkv_t, prob_t, gm_t[...], grads.at[0])

    def back(b, weight_ref):
        def product(lanes):
            total = dot_nn(grads[b, 0], weight_ref[0:cols, lanes])
            for part in range(1, 3):
                total += dot_nn(grads[b, part], weight_ref[part * cols : (part + 1) * cols, lanes])
            return total

        return product

    partial_and_send(1, back(0, wt_ref))
    transposed(ti, lt_ti)
    wait(mix_ts, hd_r.at[1])
    weight_terms(0, lt_ti, lt_go, mix_ts)
    switch(1)
    weights_y(0)
    sum_z(1, tg, tge, tgg, go_ref)
    loaded(7)
    weights_z(0)
    gather_x(1, tg, tge, tgg)

    grad_mixed_s = dot_nt(tg[...], wos_ref[...]).astype(BF16)
    attend_back(qkv_s, prob_s, grad_mixed_s, grads.at[1])
    partial_and_send(2, back(1, ws_ref))
    transposed(tg, lt_tg)
    weight_terms(1, lt_x, lt_tg, mix_s)

    def exchange(j):
        sum_x(2, j)
        send(sb.at[2, j], eb.at[j], eb_s.at[j], eb_r.at[j], (dp, s, (1 - zh) * z.nx + xi))
        leaving.append((eb, (j,), eb_s, (j,), None if j < z.reg else True))

    def finish(j, k_sem):
        wait(eb.at[j], eb_r.at[j])
        lanes = tile_lanes(xi, j) if j < z.reg else last
        total = tg[:, lanes].astype(F32) + (sb[2, j].astype(F32) + eb[j].astype(F32))
        out_ref[:, lanes] = total.astype(BF16)
        for k in range(z.nx - 1):
            send(out_ref.at[:, lanes], out_ref.at[:, lanes], ag_s.at[2, j], ag_r.at[2, j, k_sem(k)], at_x(k))
        leaving.append((rx, (2, j,), ag_s, (2, j,), None if j < z.reg else True))

    for j in range(z.reg):
        exchange(j)

    @pl.when(is_owner)
    def _():
        exchange(z.reg)

    weights_y(1)
    weights_z(1)
    for j in range(z.reg):
        finish(j, lambda k: k)

    @pl.when(is_owner)
    def _():
        finish(z.reg, lambda k: 0)

    weights_end(0, wt_out)
    for k in range(z.nx - 1):
        who = (xi - k - 1 + z.nx) % z.nx
        for j in range(z.reg):
            wait(out_ref.at[:, tile_lanes(who, j)], ag_r.at[2, j, k])

    @pl.when(jnp.logical_not(is_owner))
    def _():
        wait(out_ref.at[:, last], ag_r.at[2, z.reg, 0])

    weights_end(1, ws_out)

    on_leaving()


def finish_kernel(z, grad_ref, wt_ref, ws_ref, grad_out, qkv_s_out, out_s_out, qkv_t_out, out_t_out):
    grad_out[...] = grad_ref[...]
    for w_ref, qkv_out, out_out in ((ws_ref, qkv_s_out, out_s_out), (wt_ref, qkv_t_out, out_t_out)):
        rows = [w_ref[i * z.rr : (i + 1) * z.rr, :] for i in range(z.wide // LANES)]
        rows = jnp.concatenate(rows, axis=1)
        for part in range(3):
            qkv_out[:, part, :] = rows[:, part * z.cols : (part + 1) * z.cols]
        out_out[...] = rows[:, 3 * z.cols : 4 * z.cols]


def finish(z, *arrays):
    vmem = pl.BlockSpec(memory_space=pltpu.VMEM)
    qkv = jax.ShapeDtypeStruct((z.rr, 3, z.cols), F32)
    out = jax.ShapeDtypeStruct((z.rr, z.cols), F32)
    return pl.pallas_call(
        functools.partial(finish_kernel, z),
        out_shape=(jax.ShapeDtypeStruct((z.tokens, z.width), BF16), qkv, out, qkv, out),
        in_specs=[vmem] * 3,
        out_specs=[vmem] * 5,
    )(*arrays)


def run(z, *arrays):
    n, width, cols = z.tokens, z.width, z.cols
    chunks = z.reg + 1
    dma = pltpu.SemaphoreType.DMA
    vmem = pltpu.VMEM
    shared = z.per * ROWS
    return pl.pallas_call(
        functools.partial(kernel, z),
        out_shape=(
            jax.ShapeDtypeStruct((n, width), BF16),
            jax.ShapeDtypeStruct((z.packed, LANES), F32),
            jax.ShapeDtypeStruct((z.packed, LANES), F32),
        ),
        in_specs=[pl.BlockSpec(memory_space=pl.ANY)] * len(arrays),
        out_specs=[pl.BlockSpec(memory_space=pltpu.VMEM)] * 3,
        scratch_shapes=[
            vmem((n, width), BF16), vmem((3 * cols, width), BF16), vmem((cols, width), BF16),
            vmem((n, width), BF16), vmem((3 * cols, width), BF16), vmem((cols, width), BF16),
            vmem((width, width), BF16), vmem((z.nzl * z.packed, z.wide // LANES * z.y_rows), BF16), dma((8,)),
            vmem((3, n, cols), BF16), vmem((3, n, cols), BF16),
            vmem((2, n, n), F32), vmem((2, n, n), F32),
            vmem((n, cols), BF16), vmem((n, cols), BF16), vmem((n, cols), BF16),
            vmem((n, cols), BF16), vmem((n, cols), BF16),
            vmem((2, 3, n, cols), BF16),
            vmem((3, n, width), BF16),
            vmem((3, chunks, z.nx - 1, n, LANES), BF16),
            vmem((3, chunks, n, LANES), BF16),
            vmem((2, z.reg, 2 * n, LANES), BF16),
            vmem((2, 2 * shared, LANES), BF16),
            vmem((chunks, n, LANES), BF16),
            vmem((n, width), BF16), vmem((shared, LANES), BF16), vmem((z.nx - 1, shared, LANES), BF16),
            vmem((n, width), BF16), vmem((shared, LANES), BF16), vmem((z.nx - 1, shared, LANES), BF16),
            vmem((width, n), BF16), vmem((width, n), BF16), vmem((width, n), BF16), vmem((width, n), BF16),
            vmem((2, width, z.wide), BF16), vmem((2, z.core_rows, z.wide), BF16),
            vmem((2, z.core_rows, z.wide), BF16), vmem((2, z.ny - 1, z.y_rows, z.wide), BF16),
            vmem((2, z.nzl * z.packed, LANES), BF16), vmem((2, z.nzl, z.packed, LANES), BF16),
            dma((3, chunks)), dma((3, chunks)),
            dma((2, chunks)), dma((2, chunks)),
            dma((3, chunks)), dma((3, chunks, z.nx - 1)),
            dma((2,)), dma((2,)),
            dma((chunks,)), dma((chunks,)),
            dma((2, 3)), dma((2, 3)),
        ],
        compiler_params=pltpu.CompilerParams(
            collective_id=0, has_side_effects=True, vmem_limit_bytes=56 * 1024 * 1024
        ),
    )(*arrays)


def solution(mesh):
    def on_device(spatial_input, out_grad, qkv_spatial, out_spatial, qkv_temporal, out_temporal):
        width = spatial_input.shape[-1]
        tokens = spatial_input.shape[-2]
        z = Sizes(mesh.shape, tokens, width)
        cols = z.cols

        def flat(weight):
            return weight.transpose(1, 2, 0).reshape(3 * cols, width)

        grad, wt, ws = run(
            z,
            spatial_input.reshape(tokens, width), flat(qkv_spatial), out_spatial,
            out_grad.reshape(tokens, width), flat(qkv_temporal), out_temporal,
            row_order(z), row_pack(z),
        )
        grad, qkv_s_grad, out_s_grad, qkv_t_grad, out_t_grad = finish(z, grad, wt, ws)
        return grad.reshape(spatial_input.shape), qkv_s_grad, out_s_grad.T, qkv_t_grad, out_t_grad.T

    placed = (
        P("dp", "sp", None, None),
        P("dp", "sp", None, None),
        P(None, None, "tp"),
        P("tp", None),
        P(None, None, "tp"),
        P("tp", None),
    )
    return jax.shard_map(
        on_device,
        mesh=mesh,
        in_specs=placed,
        out_specs=(
            P("dp", "sp", None, None),
            P(("sp", "dp"), None, "tp"),
            P("tp", ("sp", "dp")),
            P(("sp", "dp"), None, "tp"),
            P("tp", ("sp", "dp")),
        ),
        check_vma=False,
    )
```

```python
import functools

import jax
import jax.numpy as jnp
import numpy as np
from jax import lax
from jax.experimental import pallas as pl
from jax.experimental.pallas import tpu as pltpu
from jax.sharding import PartitionSpec as P

HEAD_DIM = 72
LANES = 128
ROWS = 16
MESH = pl.DeviceIdType.MESH
F32, BF16 = jnp.float32, jnp.bfloat16


def dot_nn(left, right):
    return lax.dot_general(left, right, (((1,), (0,)), ((), ())), preferred_element_type=F32)


def dot_nt(left, right):
    return lax.dot_general(left, right, (((1,), (1,)), ((), ())), preferred_element_type=F32)


def dot_tn(left, right):
    return lax.dot_general(left, right, (((0,), (0,)), ((), ())), preferred_element_type=F32)


class Sizes:
    def __init__(self, mesh_shape, tokens, width):
        self.ny, self.ns = mesh_shape["dp"], mesh_shape["sp"]
        self.nx = mesh_shape["tp"] // 2
        self.nzl = self.ns // 2
        self.tokens, self.width = tokens, width
        self.tiles = width // LANES
        self.reg = self.tiles // self.nx
        assert self.tiles == self.reg * self.nx + 1
        self.per = self.ns // self.nx
        self.cols = 2 * HEAD_DIM
        self.wide = -(-(4 * self.cols) // LANES) * LANES
        self.core_rows = width // 2
        self.y_rows = self.core_rows // self.ny
        self.rr = width // (self.ns * self.ny)
        self.packed = -(-(self.wide // LANES) * self.rr // 16) * 16


def row_order(z):
    order = np.arange(z.width).reshape(z.nzl, 2, z.ny, z.rr).transpose(1, 2, 0, 3).reshape(-1)
    onehot = np.zeros((z.width, z.width), np.float32)
    onehot[np.arange(z.width), order] = 1.0
    return onehot.astype(jnp.bfloat16)


def row_pack(z):
    tiles = z.wide // LANES
    onehot = np.zeros((z.nzl, z.packed, tiles, z.nzl, z.rr), np.float32)
    for chip in range(z.nzl):
        for tile in range(tiles):
            for row in range(z.rr):
                onehot[chip, tile * z.rr + row, tile, chip, row] = 1.0
    return onehot.reshape(z.nzl * z.packed, tiles * z.y_rows).astype(jnp.bfloat16)


def kernel(
    z,
    x_hbm, ws_hbm, wos_hbm, go_hbm, wt_hbm, wot_hbm, order_hbm, pack_hbm,
    out_ref, wt_out, ws_out,
    x_ref, ws_ref, wos_ref, go_ref, wt_ref, wot_ref, order_ref, pack_ref, load_sems,
    qkv_s, qkv_t, prob_s, prob_t, mix_s, mix_t, mix_ts, gm_s, gm_t, grads,
    pb, pbl, rx, rxl, sb, sbl, zb, ze, spare, eb, ebl, oute, outg,
    ti, tie, tig, tg, tge, tgg,
    lt_x, lt_ti, lt_go, lt_tg,
    term, term_in, yb, yr, zw, zr,
    rx_s, rx_r, zb_s, zb_r, ag_s, ag_r, hd_s, hd_r, eb_s, eb_r,
    w_s, w_r,
):
    n = z.tokens
    cols = z.cols
    factor = HEAD_DIM ** (-0.5)
    dp, s, t = lax.axis_index("dp"), lax.axis_index("sp"), lax.axis_index("tp")
    zh, xi = t // z.nx, t % z.nx
    zl, core = s // 2, s % 2
    last = pl.ds((z.tiles - 1) * LANES, LANES)

    def at_x(k):
        return (dp, s, zh * z.nx + (xi + k + 1) % z.nx)

    def at_z(i):
        away, way = z.nzl - i // 4, 1 - 2 * ((i % 4) // 2)
        chip = (zh * z.nzl + zl + way * away + 2 * z.nzl) % (2 * z.nzl)
        to = (chip % z.nzl) * 2 + (core + i + 1) % 2
        return to, (dp, to, (chip // z.nzl) * z.nx + xi)

    def send(src, dst, ssem, rsem, dev):
        pltpu.make_async_remote_copy(
            src_ref=src, dst_ref=dst, send_sem=ssem, recv_sem=rsem, device_id=dev, device_id_type=MESH
        ).start()

    def wait(ref, sem):
        pltpu.make_async_copy(ref, ref, sem).wait()

    leaving = []

    def on_leaving():
        for ref, place, sem, sem_place in leaving:
            wait(ref.at[place] if place else ref, sem.at[sem_place])

    sent_z = pl.ds(0, (2 * z.ns - 1) * ROWS)
    sent_sp = pl.ds(0, (z.ns - 1) * ROWS)

    def tile_lanes(who, j, count=1):
        return pl.ds(pl.multiple_of((who * z.reg + j) * LANES, LANES), count * LANES)

    def rows_of(i, base=0):
        return pl.ds(pl.multiple_of(base + i * ROWS, ROWS), ROWS)

    barrier = pltpu.get_barrier_semaphore()
    def greet(i, carry):
        pl.semaphore_signal(barrier, inc=1, device_id=at_z(i)[1], device_id_type=MESH)
        return carry

    lax.fori_loop(2, 2 * z.ns + 1, greet, 0)
    for k in range(z.nx - 1):
        pl.semaphore_signal(barrier, inc=1, device_id=at_x(k), device_id_type=MESH)
    for k in range(z.ny - 1):
        pl.semaphore_signal(barrier, inc=1, device_id=((dp + k + 1) % z.ny, s, t), device_id_type=MESH)

    loads = (
        (x_hbm, x_ref), (ws_hbm, ws_ref), (wos_hbm, wos_ref), (wot_hbm, wot_ref), (go_hbm, go_ref),
        (order_hbm, order_ref), (wt_hbm, wt_ref), (pack_hbm, pack_ref),
    )
    for i, (src, dst) in enumerate(loads):
        pltpu.make_async_copy(src, dst, load_sems.at[i]).start()

    def loaded(*which):
        for i in which:
            wait(loads[i][1], load_sems.at[i])

    def switch_heads(b, src, dst):
        pltpu.make_async_copy(src.at[rows_of(s)], dst.at[rows_of(s)], hd_r.at[b]).start()

        def one(i, carry):
            to = (s + i) % z.ns
            send(src.at[rows_of(to)], dst.at[rows_of(s)], hd_s.at[b], hd_r.at[b], (dp, to, t))
            return carry

        lax.fori_loop(1, z.ns, one, 0)
        leaving.append((dst, (sent_sp,), hd_s, (b,)))

    first_head = lax.broadcasted_iota(jnp.int32, (n, cols), 1) < HEAD_DIM

    def one_head(rows, h):
        keep = first_head if h == 0 else jnp.logical_not(first_head)
        return jnp.where(keep, rows.astype(F32), 0.0).astype(BF16)

    def both_heads(pair):
        return jnp.where(first_head, pair[0], pair[1])

    def project(rows, weight_ref, qkv_ref):
        for part in range(3):
            qkv_ref[part] = dot_nt(rows, weight_ref[part * cols : (part + 1) * cols, :]).astype(BF16)

    def attend(qkv_ref, prob_ref, mix_ref, same):
        q, k, v = qkv_ref[0], qkv_ref[1], qkv_ref[2]
        mixed = []
        for h in range(2):
            scores = dot_nt(one_head(q, h), k) * factor
            if same is not None:
                scores = jnp.where(same, scores, -1e30)
            e = jnp.exp(scores - jnp.max(scores, axis=-1, keepdims=True))
            probs = e / jnp.sum(e, axis=-1, keepdims=True)
            prob_ref[h] = probs
            mixed.append(dot_nn(probs.astype(BF16), v))
        mix_ref[...] = both_heads(mixed).astype(BF16)

    def attend_back(qkv_ref, prob_ref, grad_mixed, grads_ref):
        q, k, v = qkv_ref[0], qkv_ref[1], qkv_ref[2]
        dq, dk, dv = [], [], []
        for h in range(2):
            probs = prob_ref[h]
            dp_ = dot_nt(one_head(grad_mixed, h), v)
            centre = jnp.sum(dp_ * probs, axis=-1, keepdims=True)
            ds = (probs * (dp_ - centre) * factor).astype(BF16)
            dq.append(dot_nn(ds, k))
            dk.append(dot_tn(ds, q))
            dv.append(dot_tn(probs.astype(BF16), grad_mixed))
        for part, pair in enumerate((dq, dk, dv)):
            grads_ref[part] = both_heads(pair).astype(BF16)

    def transposed(rows_ref, lt_ref):
        step = z.width // 2

        def one(i, carry):
            at = pl.ds(pl.multiple_of(i * step, 16), step)
            lt_ref[at, :] = dot_nt(order_ref[at, :], rows_ref[...]).astype(BF16)
            return carry

        lax.fori_loop(0, z.width // step, one, 0)

    def send_x(p, j):
        for k in range(z.nx - 1):
            to = (xi + k + 1) % z.nx
            send(pb.at[p, :, tile_lanes(to, j)], rx.at[p, j, k], rx_s.at[p, j], rx_r.at[p, j], at_x(k))
        leaving.append((rx, (p, j), rx_s, (p, j)))

    share = z.per * ROWS

    def class_of(x_place):
        return (x_place - s + z.ns) % z.nx

    def share_rows(x_place):
        return pl.ds(pl.multiple_of(class_of(x_place) * share, ROWS), share)

    def member(x_place, i):
        return class_of(x_place) + z.nx * i

    def send_x_last(p):
        for k in range(z.nx - 1):
            to = (xi + k + 1) % z.nx
            send(pbl.at[p, share_rows(to)], rxl.at[p, k], rx_s.at[p, z.reg], rx_r.at[p, z.reg], at_x(k))
        leaving.append((rxl, (p,), rx_s, (p, z.reg)))

    def partial_and_send(p, product):
        for j in range(z.reg):
            for who in range(z.nx):
                lanes = slice((who * z.reg + j) * LANES, (who * z.reg + j + 1) * LANES)
                pb[p, :, lanes] = product(lanes).astype(BF16)
            send_x(p, j)
        tile = product(slice((z.tiles - 1) * LANES, z.tiles * LANES)).astype(BF16)
        for b in range(z.ns):
            place = ((b % z.nx) * z.per + b // z.nx) * ROWS
            pbl[p, place : place + ROWS, :] = tile[b * ROWS : (b + 1) * ROWS, :]
        send_x_last(p)

    def sum_x(p, j, extra=None):
        wait(rx.at[p, j], rx_r.at[p, j])
        lanes = tile_lanes(xi, j)
        total = pb[p, :, lanes].astype(F32)
        for k in range(z.nx - 1):
            total += rx[p, j, k].astype(F32)
        if extra is not None:
            total += extra(slice(None), lanes)
        sb[p, j] = total.astype(BF16)

    def sum_x_last(p, extra=None):
        wait(rxl.at[p], rx_r.at[p, z.reg])
        total = pbl[p, share_rows(xi)].astype(F32)
        for k in range(z.nx - 1):
            total += rxl[p, k].astype(F32)
        if extra is not None:
            total += jnp.concatenate([extra(rows_of(member(xi, i)), last) for i in range(z.per)], axis=0)
        sbl[p] = total.astype(BF16)

    def send_z(p, j):
        pltpu.make_async_copy(sb.at[p, j, rows_of(s)], zb.at[p, j, rows_of(s, zh * n)], zb_r.at[p, j]).start()

        def one(i, carry):
            to, dev = at_z(i)
            send(sb.at[p, j, rows_of(to)], zb.at[p, j, rows_of(s, zh * n)], zb_s.at[p, j], zb_r.at[p, j], dev)
            return carry

        lax.fori_loop(2, 2 * z.ns + 1, one, 0)
        leaving.append((zb, (p, 0, sent_z), zb_s, (p, j)))

    def send_z_last(p):
        dst = ze.at[p, rows_of(s // z.nx, zh * share)]
        for i in range(z.per):
            to = member(xi, i)
            src = sbl.at[p, i * ROWS : (i + 1) * ROWS]
            send(src, dst, zb_s.at[p, z.reg], zb_r.at[p, z.reg], (dp, to, (1 - zh) * z.nx + xi))

            @pl.when(to != s)
            def _():
                send(src, dst, zb_s.at[p, z.reg], zb_r.at[p, z.reg], (dp, to, t))

            @pl.when(to == s)
            def _():
                pltpu.make_async_copy(src, dst, zb_r.at[p, z.reg]).start()
                pltpu.make_async_copy(src, spare.at[p], zb_s.at[p, z.reg]).start()

        leaving.append((ze, (p,), zb_s, (p, z.reg)))

    def switch(p, extra=None):
        for j in range(z.reg):
            sum_x(p, j, extra)
            send_z(p, j)
        sum_x_last(p, extra)
        send_z_last(p)

    def sum_z(p, full, mine, others, extra=None):
        for j in range(z.reg):
            wait(zb.at[p, j], zb_r.at[p, j])
            lanes = tile_lanes(xi, j)
            total = zb[p, j, 0:n].astype(F32) + zb[p, j, n : 2 * n].astype(F32)
            if extra is not None:
                total += extra[:, lanes].astype(F32)
            full[:, lanes] = total.astype(BF16)
            for k in range(z.nx - 1):
                send(full.at[:, lanes], full.at[:, lanes], ag_s.at[p, j], ag_r.at[p, j, k], at_x(k))
            leaving.append((rx, (p, j), ag_s, (p, j)))
        wait(ze.at[p], zb_r.at[p, z.reg])
        total = ze[p, 0:share].astype(F32) + ze[p, share : 2 * share].astype(F32)
        if extra is not None:
            total += jnp.concatenate([extra[rows_of(member(xi, i)), last] for i in range(z.per)], axis=0).astype(F32)
        mine[...] = total.astype(BF16)
        for k in range(z.nx - 1):
            send(mine, others.at[k], ag_s.at[p, z.reg], ag_r.at[p, z.reg, k], at_x(k))
        leaving.append((others, (), ag_s, (p, z.reg)))

    def place_last(full, block, who):
        for i in range(z.per):
            full[rows_of(member(who, i)), last] = block[i * ROWS : (i + 1) * ROWS, :]

    def gather_x(p, full, mine, others):
        place_last(full, mine, xi)
        for k in range(z.nx - 1):
            who = (xi - k - 1 + z.nx) % z.nx
            for j in range(z.reg):
                wait(full.at[:, tile_lanes(who, j)], ag_r.at[p, j, k])
            wait(others.at[k], ag_r.at[p, z.reg, k])
            place_last(full, others.at[k], who)

    def weight_terms(b, lt_qkv, lt_out, mix_ref):
        tail = z.wide - LANES * (3 * cols // LANES)
        base = z.wide - tail
        packed = jnp.concatenate(
            [grads[b, 0], grads[b, 1], grads[b, 2], jnp.zeros((n, z.wide - 3 * cols), BF16)], axis=1
        )
        placed = jnp.concatenate(
            [jnp.zeros((n, 3 * cols - base), BF16), mix_ref[...], jnp.zeros((n, z.wide - 4 * cols), BF16)], axis=1
        )
        step = z.width // 2

        def one(i, carry):
            at = pl.ds(pl.multiple_of(i * step, 16), step)
            left, left_out = lt_qkv[at, :], lt_out[at, :]
            term[b, at, 0:base] = dot_nn(left, packed[:, 0:base]).astype(BF16)
            term[b, at, base : z.wide] = (dot_nn(left, packed[:, base:]) + dot_nn(left_out, placed)).astype(BF16)
            return carry

        lax.fori_loop(0, z.width // step, one, 0)
        away = pl.ds(pl.multiple_of((1 - core) * z.core_rows, 16), z.core_rows)
        send(term.at[b, away], term_in.at[b], w_s.at[b, 0], w_r.at[b, 0], (dp, s + 1 - 2 * core, t))
        leaving.append((term_in, (b,), w_s, (b, 0,)))

    def weights_y(b):
        wait(term_in.at[b], w_r.at[b, 0])
        here = pl.ds(pl.multiple_of(core * z.core_rows, 16), z.core_rows)
        yb[b] = (term[b, here].astype(F32) + term_in[b].astype(F32)).astype(BF16)
        for k in range(z.ny - 1):
            to = (dp + k + 1) % z.ny
            src = yb.at[b, pl.ds(pl.multiple_of(to * z.y_rows, 16), z.y_rows)]
            send(src, yr.at[b, k], w_s.at[b, 1], w_r.at[b, 1], (to, s, t))
        leaving.append((yr, (b,), w_s, (b, 1,)))

    def weights_z(b):
        wait(yr.at[b], w_r.at[b, 1])
        total = yb[b, pl.ds(pl.multiple_of(dp * z.y_rows, 16), z.y_rows)].astype(F32)
        for k in range(z.ny - 1):
            total += yr[b, k].astype(F32)
        total = total.astype(BF16)
        stacked = jnp.concatenate([total[:, i : i + LANES] for i in range(0, z.wide, LANES)], axis=0)
        zw[b] = dot_nn(pack_ref[...], stacked).astype(BF16)

        def block(i):
            return pl.ds(pl.multiple_of(i * z.packed, 16), z.packed)

        pltpu.make_async_copy(zw.at[b, block(zl)], zr.at[b, zl], w_r.at[b, 2]).start()
        for k in range(z.nzl - 1):
            to = (zl + k + 1) % z.nzl
            send(zw.at[b, block(to)], zr.at[b, zl], w_s.at[b, 2], w_r.at[b, 2], (dp, 2 * to + core, t))
        leaving.append((zr, (b, pl.ds(0, z.nzl - 1),), w_s, (b, 2,)))

    def weights_end(b, w_out):
        wait(zr.at[b], w_r.at[b, 2])
        total = zr[b, 0].astype(F32)
        for k in range(1, z.nzl):
            total += zr[b, k].astype(F32)
        w_out[...] = total

    loaded(0, 1)
    project(x_ref[...], ws_ref, qkv_s)
    attend(qkv_s, prob_s, mix_s, None)
    loaded(2)
    pl.semaphore_wait(barrier, (z.nx - 1) + (z.ny - 1) + (2 * z.ns - 1))
    partial_and_send(0, lambda lanes: dot_nn(mix_s[...], wos_ref[:, lanes]))
    loaded(3, 4)
    gm_s[...] = dot_nt(go_ref[...], wot_ref[...]).astype(BF16)

    switch_heads(0, gm_s, gm_t)

    def add_input(rows, lanes):
        return x_ref[rows, lanes].astype(F32) * jnp.where(zh == 0, 1.0, 0.0)

    switch(0, add_input)
    loaded(5)
    transposed(x_ref, lt_x)
    transposed(go_ref, lt_go)
    sum_z(0, ti, tie, tig)
    loaded(6)
    gather_x(0, ti, tie, tig)

    rows_i = lax.broadcasted_iota(jnp.int32, (n, n), 0)
    cols_i = lax.broadcasted_iota(jnp.int32, (n, n), 1)
    same = (rows_i & (ROWS - 1)) == (cols_i & (ROWS - 1))
    project(ti[...], wt_ref, qkv_t)
    attend(qkv_t, prob_t, mix_t, same)
    switch_heads(1, mix_t, mix_ts)
    wait(gm_t, hd_r.at[0])
    attend_back(qkv_t, prob_t, gm_t[...], grads.at[0])

    def back(b, weight_ref):
        def product(lanes):
            total = dot_nn(grads[b, 0], weight_ref[0:cols, lanes])
            for part in range(1, 3):
                total += dot_nn(grads[b, part], weight_ref[part * cols : (part + 1) * cols, lanes])
            return total

        return product

    partial_and_send(1, back(0, wt_ref))
    transposed(ti, lt_ti)
    wait(mix_ts, hd_r.at[1])
    weight_terms(0, lt_ti, lt_go, mix_ts)
    switch(1)
    weights_y(0)
    sum_z(1, tg, tge, tgg, go_ref)
    loaded(7)
    weights_z(0)
    gather_x(1, tg, tge, tgg)

    grad_mixed_s = dot_nt(tg[...], wos_ref[...]).astype(BF16)
    attend_back(qkv_s, prob_s, grad_mixed_s, grads.at[1])
    partial_and_send(2, back(1, ws_ref))
    transposed(tg, lt_tg)
    weight_terms(1, lt_x, lt_tg, mix_s)

    def exchange(src, dst, j):
        send(src, dst, eb_s.at[j], eb_r.at[j], (dp, s, (1 - zh) * z.nx + xi))

    for j in range(z.reg):
        sum_x(2, j)
        exchange(sb.at[2, j], eb.at[j], j)
        leaving.append((eb, (j,), eb_s, (j,)))
    sum_x_last(2)
    exchange(sbl.at[2], ebl, z.reg)
    leaving.append((ebl, (), eb_s, (z.reg,)))
    weights_y(1)
    for j in range(z.reg):
        if j == 1:
            weights_z(1)
        wait(eb.at[j], eb_r.at[j])
        lanes = tile_lanes(xi, j)
        total = tg[:, lanes].astype(F32) + (sb[2, j].astype(F32) + eb[j].astype(F32))
        out_ref[:, lanes] = total.astype(BF16)
        for k in range(z.nx - 1):
            send(out_ref.at[:, lanes], out_ref.at[:, lanes], ag_s.at[2, j], ag_r.at[2, j, k], at_x(k))
        leaving.append((rx, (2, j), ag_s, (2, j)))
    wait(ebl, eb_r.at[z.reg])
    total = jnp.concatenate([tg[rows_of(member(xi, i)), last] for i in range(z.per)], axis=0).astype(F32)
    oute[...] = (total + (sbl[2].astype(F32) + ebl[...].astype(F32))).astype(BF16)
    for k in range(z.nx - 1):
        send(oute, outg.at[k], ag_s.at[2, z.reg], ag_r.at[2, z.reg, k], at_x(k))
    leaving.append((outg, (), ag_s, (2, z.reg)))
    weights_end(0, wt_out)
    gather_x(2, out_ref, oute, outg)
    weights_end(1, ws_out)

    on_leaving()


def finish_kernel(z, grad_ref, wt_ref, ws_ref, grad_out, qkv_s_out, out_s_out, qkv_t_out, out_t_out):
    grad_out[...] = grad_ref[...]
    for w_ref, qkv_out, out_out in ((ws_ref, qkv_s_out, out_s_out), (wt_ref, qkv_t_out, out_t_out)):
        rows = [w_ref[i * z.rr : (i + 1) * z.rr, :] for i in range(z.wide // LANES)]
        rows = jnp.concatenate(rows, axis=1)
        for part in range(3):
            qkv_out[:, part, :] = rows[:, part * z.cols : (part + 1) * z.cols]
        out_out[...] = rows[:, 3 * z.cols : 4 * z.cols]


def finish(z, *arrays):
    vmem = pl.BlockSpec(memory_space=pltpu.VMEM)
    qkv = jax.ShapeDtypeStruct((z.rr, 3, z.cols), F32)
    out = jax.ShapeDtypeStruct((z.rr, z.cols), F32)
    return pl.pallas_call(
        functools.partial(finish_kernel, z),
        out_shape=(jax.ShapeDtypeStruct((z.tokens, z.width), BF16), qkv, out, qkv, out),
        in_specs=[vmem] * 3,
        out_specs=[vmem] * 5,
    )(*arrays)


def run(z, *arrays):
    n, width, cols = z.tokens, z.width, z.cols
    chunks = z.reg + 1
    dma = pltpu.SemaphoreType.DMA
    vmem = pltpu.VMEM
    shared = z.per * ROWS
    return pl.pallas_call(
        functools.partial(kernel, z),
        out_shape=(
            jax.ShapeDtypeStruct((n, width), BF16),
            jax.ShapeDtypeStruct((z.packed, LANES), F32),
            jax.ShapeDtypeStruct((z.packed, LANES), F32),
        ),
        in_specs=[pl.BlockSpec(memory_space=pl.ANY)] * len(arrays),
        out_specs=[pl.BlockSpec(memory_space=pltpu.VMEM)] * 3,
        scratch_shapes=[
            vmem((n, width), BF16), vmem((3 * cols, width), BF16), vmem((cols, width), BF16),
            vmem((n, width), BF16), vmem((3 * cols, width), BF16), vmem((cols, width), BF16),
            vmem((width, width), BF16), vmem((z.nzl * z.packed, z.wide // LANES * z.y_rows), BF16), dma((8,)),
            vmem((3, n, cols), BF16), vmem((3, n, cols), BF16),
            vmem((2, n, n), F32), vmem((2, n, n), F32),
            vmem((n, cols), BF16), vmem((n, cols), BF16), vmem((n, cols), BF16),
            vmem((n, cols), BF16), vmem((n, cols), BF16),
            vmem((2, 3, n, cols), BF16),
            vmem((3, n, width), BF16), vmem((3, n, LANES), BF16),
            vmem((3, z.reg, z.nx - 1, n, LANES), BF16), vmem((3, z.nx - 1, shared, LANES), BF16),
            vmem((3, z.reg, n, LANES), BF16), vmem((3, shared, LANES), BF16),
            vmem((2, z.reg, 2 * n, LANES), BF16),
            vmem((2, 2 * shared, LANES), BF16), vmem((2, ROWS, LANES), BF16),
            vmem((z.reg, n, LANES), BF16), vmem((shared, LANES), BF16),
            vmem((shared, LANES), BF16), vmem((z.nx - 1, shared, LANES), BF16),
            vmem((n, width), BF16), vmem((shared, LANES), BF16), vmem((z.nx - 1, shared, LANES), BF16),
            vmem((n, width), BF16), vmem((shared, LANES), BF16), vmem((z.nx - 1, shared, LANES), BF16),
            vmem((width, n), BF16), vmem((width, n), BF16), vmem((width, n), BF16), vmem((width, n), BF16),
            vmem((2, width, z.wide), BF16), vmem((2, z.core_rows, z.wide), BF16),
            vmem((2, z.core_rows, z.wide), BF16), vmem((2, z.ny - 1, z.y_rows, z.wide), BF16),
            vmem((2, z.nzl * z.packed, LANES), BF16), vmem((2, z.nzl, z.packed, LANES), BF16),
            dma((3, chunks)), dma((3, chunks)),
            dma((2, chunks)), dma((2, chunks)),
            dma((3, chunks)), dma((3, chunks, z.nx - 1)),
            dma((2,)), dma((2,)),
            dma((chunks,)), dma((chunks,)),
            dma((2, 3)), dma((2, 3)),
        ],
        compiler_params=pltpu.CompilerParams(
            collective_id=0, has_side_effects=True, vmem_limit_bytes=56 * 1024 * 1024
        ),
    )(*arrays)


def solution(mesh):
    def on_device(spatial_input, out_grad, qkv_spatial, out_spatial, qkv_temporal, out_temporal):
        width = spatial_input.shape[-1]
        tokens = spatial_input.shape[-2]
        z = Sizes(mesh.shape, tokens, width)
        cols = z.cols

        def flat(weight):
            return weight.transpose(1, 2, 0).reshape(3 * cols, width)

        grad, wt, ws = run(
            z,
            spatial_input.reshape(tokens, width), flat(qkv_spatial), out_spatial,
            out_grad.reshape(tokens, width), flat(qkv_temporal), out_temporal,
            row_order(z), row_pack(z),
        )
        grad, qkv_s_grad, out_s_grad, qkv_t_grad, out_t_grad = finish(z, grad, wt, ws)
        return grad.reshape(spatial_input.shape), qkv_s_grad, out_s_grad.T, qkv_t_grad, out_t_grad.T

    placed = (
        P("dp", "sp", None, None),
        P("dp", "sp", None, None),
        P(None, None, "tp"),
        P("tp", None),
        P(None, None, "tp"),
        P("tp", None),
    )
    return jax.shard_map(
        on_device,
        mesh=mesh,
        in_specs=placed,
        out_specs=(
            P("dp", "sp", None, None),
            P(("sp", "dp"), None, "tp"),
            P("tp", ("sp", "dp")),
            P(("sp", "dp"), None, "tp"),
            P("tp", ("sp", "dp")),
        ),
        check_vma=False,
    )
```
